768 devices in a mesh: gx: 24 (over z, core), gy: 4 (over x), gz: 8 (over y).
Axes of the slice: x: 4, y: 8, z: 12, core: 2. Of those that a mesh axis runs over, the one named last changes fastest.
Arguments:
- design: float32 [96, 32, 1024], P('gx', 'gy', 'gz'), may hold values from 0.05 to 1
- passive: int32 [96, 32, 1024], P('gx', 'gy', 'gz'), may hold values from 0 to 2, as said below
- fixed: int32 [96, 32, 1024], P('gx', 'gy', 'gz'), may hold values 0 or 1
- state: float32 [3, 96, 32, 1024], P(None, 'gx', 'gy', 'gz'), may hold values from -6 to 6
- adjoint: float32 [3, 96, 32, 1024], P(None, 'gx', 'gy', 'gz'), may hold values from -6 to 6
- resid: float32 [3, 96, 32, 1024], P(None, 'gx', 'gy', 'gz'), may hold values from -10 to 10
Outputs:
- adjoint_new: float32 [3, 96, 32, 1024], P(None, 'gx', 'gy', 'gz')
- resid_new: float32 [3, 96, 32, 1024], P(None, 'gx', 'gy', 'gz')
- design_grad: float32 [96, 32, 1024], P('gx', 'gy', 'gz')
The draws below stay inside these ranges and needn't reach their ends.
Inputs may be any that keep to these rules, and one draw needn't show every extreme that they name: `passive`: 0 marks a design element, 1 an element held void, 2 one held solid.
All inputs are finite; a program needn't handle non-finite values. No bound on the sum of `fixed` on one device may be relied on, other than what follows from the above.
Results may differ from the reference program's by a relative error of at most 0.0003.
Values sent between devices are 32-bit elements; how exact they have to be, the bound alone decides.
A program may use at most 32 MiB of HBM per device.

```python
import math
import jax
import jax.numpy as jnp
from jax import lax

CX = 4
CY = 8
CZ = 128
NX = 96
NY = 32
NZ = 1024


def draw_passive(key, part):
    key = jax.random.fold_in(key, 3)
    code = jax.random.randint(key, (NX, NY, NZ), 0, 20)
    return jnp.where(code < 2, 1, jnp.where(code < 4, 2, 0)).astype(jnp.int32)


def draw_resid(key, part):
    key = jax.random.fold_in(key, 5)
    noise_key, level_key, phase_key = jax.random.split(key, 3)
    blocks = (3, NX // CX, NY // CY, NZ // CZ)
    noise = jnp.clip(jax.random.normal(noise_key, (3, NX, NY, NZ), jnp.float32), -6.0, 6.0)
    levels = jnp.exp(jax.random.uniform(level_key, blocks, jnp.float32, math.log(0.2), math.log(3.0)))
    levels = jnp.repeat(jnp.repeat(jnp.repeat(levels, CX, axis=1), CY, axis=2), CZ, axis=3)
    phases = jax.random.uniform(phase_key, (3, 3), jnp.float32, 0.0, 2.0 * math.pi)
    along_x = ((jnp.arange(NX, dtype=jnp.float32) + 0.5) / NX)[None, :, None, None]
    along_y = ((jnp.arange(NY, dtype=jnp.float32) + 0.5) / NY)[None, None, :, None]
    along_z = ((jnp.arange(NZ, dtype=jnp.float32) + 0.5) / NZ)[None, None, None, :]
    turn = 2.0 * math.pi
    wave = jnp.sin(turn * along_x + phases[:, 0, None, None, None])
    wave = wave + jnp.sin(turn * (along_y + along_z) + phases[:, 1, None, None, None])
    wave = wave + jnp.sin(turn * (along_x - 2.0 * along_z) + phases[:, 2, None, None, None])
    return (noise + levels * wave / 3.0).astype(jnp.float32)


def place_ends(values, own_key, low, high):
    dims = values.shape
    place = [jax.random.randint(jax.random.fold_in(own_key, axis), (), 0, dims[axis]) for axis in range(len(dims))]
    values = values.at[tuple(place)].set(low)
    longest = dims.index(max(dims))
    place[longest] = (place[longest] + 1) % dims[longest]
    return values.at[tuple(place)].set(high)


def block_levels(stream_key, dims, cuts, low, top_value):
    level = 1.0
    for position, shards_of in cuts:
        steps = jax.random.uniform(jax.random.fold_in(jax.random.fold_in(stream_key, 6), position), (shards_of,), jnp.float32, low / len(cuts), top_value / len(cuts))
        level = level * jnp.repeat(jnp.exp(steps), dims[position] // shards_of).reshape((-1,) + (1,) * (len(dims) - 1 - position))
    return level


def gaussian(key, extent, deviation, bound, cuts=(), held_as=jnp.bfloat16):
    gain = block_levels(key, extent, cuts, -0.22, 0.18) if cuts else 1.0
    result = jax.random.normal(key, extent, jnp.float32) * deviation * gain
    return jnp.minimum(jnp.maximum(result, -bound), bound).astype(held_as)


def setup_inputs(seed: int = 0) -> dict:
    keys = jax.random.split(jax.random.key(seed), 7)
    return {
        "design": jnp.clip(0.05 + 0.95 * jax.random.uniform(keys[0], (NX, NY, NZ), jnp.float32) ** block_levels(keys[0], (NX, NY, NZ), ((0, 24), (1, 4), (2, 8)), -0.2, 0.2), 0.05, 1.0),
        "passive": draw_passive(jax.random.fold_in(keys[6], 71), 0),
        "fixed": place_ends((jax.random.randint(keys[2], (NX, NY, NZ), 0, 16) < 1).astype(jnp.int32), jax.random.fold_in(keys[2], 1), 0, 1),
        "state": gaussian(keys[3], (3, NX, NY, NZ), 1.0, 6.0, ((1, 24), (2, 4), (3, 8)), jnp.float32),
        "adjoint": gaussian(keys[4], (3, NX, NY, NZ), 1.0, 6.0, ((1, 24), (2, 4), (3, 8)), jnp.float32),
        "resid": draw_resid(jax.random.fold_in(keys[6], 71), 0),
    }


stiff_floor = 0.001
damping = 0.6
coarse_damping = 0.5

def element_matrix():
    ratio = 0.3
    lame = ratio / ((1.0 + ratio) * (1.0 - 2.0 * ratio))
    shear = 0.5 / (1.0 + ratio)
    elastic = [[0.0] * 6 for number in range(6)]
    for i in range(3):
        for k in range(3):
            elastic[i][k] = lame
    for i in range(3):
        elastic[i][i] = elastic[i][i] + 2.0 * shear
        elastic[3 + i][3 + i] = shear
    signs = [[2 * (a >> 2 & 1) - 1, 2 * (a >> 1 & 1) - 1, 2 * (a & 1) - 1] for a in range(8)]
    point = 1.0 / math.sqrt(3.0)
    matrix = [[0.0] * 24 for number in range(24)]
    for p in (-point, point):
        for q in (-point, point):
            for s in (-point, point):
                local = [p, q, s]
                grads = [[0.0] * 3 for number in range(8)]
                for a in range(8):
                    for k in range(3):
                        value = signs[a][k] / 8.0 * 2.0
                        for m in range(3):
                            if m != k:
                                value = value * (1.0 + signs[a][m] * local[m])
                        grads[a][k] = value
                strain = [[0.0] * 24 for number in range(6)]
                for a in range(8):
                    strain[0][a] = grads[a][0]
                    strain[1][8 + a] = grads[a][1]
                    strain[2][16 + a] = grads[a][2]
                    strain[3][a] = grads[a][1]
                    strain[3][8 + a] = grads[a][0]
                    strain[4][8 + a] = grads[a][2]
                    strain[4][16 + a] = grads[a][1]
                    strain[5][a] = grads[a][2]
                    strain[5][16 + a] = grads[a][0]
                stress = [[sum((elastic[m][n] * strain[n][c] for n in range(6))) for c in range(24)] for m in range(6)]
                for r in range(24):
                    for c in range(24):
                        matrix[r][c] = matrix[r][c] + sum((strain[m][r] * stress[m][c] for m in range(6))) * 0.125
    return matrix

def corners():
    return [(a >> 2 & 1, a >> 1 & 1, a & 1) for a in range(8)]

def stencil():
    terms = []
    for i in (-1, 0, 1):
        for j in (-1, 0, 1):
            for k in (-1, 0, 1):
                terms.append((i, j, k, 2.0 - math.sqrt(i * i + j * j + k * k)))
    return terms

def smooth(field):
    padded = jnp.pad(field, 1)
    total = jnp.zeros(field.shape, jnp.float32)
    for i, j, k, weight in stencil():
        total = total + weight * padded[1 + i:1 + i + NX, 1 + j:1 + j + NY, 1 + k:1 + k + NZ]
    return total

def apply_global(field, factor, stiffness):
    padded = jnp.pad(field, ((0, 0), (0, 1), (0, 1), (0, 1)))

    def step(carry, index):
        slab = lax.dynamic_slice_in_dim(padded, index, 2, 1)
        pieces = [slab[:, i, j:j + NY, k:k + NZ] for i, j, k in corners()]
        stacked = jnp.stack(pieces, 1).reshape(24, NY * NZ)
        force = jnp.dot(stiffness, stacked, precision=lax.Precision.HIGHEST).reshape(3, 8, NY, NZ)
        force = force * lax.dynamic_index_in_dim(factor, index, 0, keepdims=False)
        force = jnp.pad(force, ((0, 0), (0, 0), (1, 0), (1, 0)))
        here = jnp.zeros((3, NY, NZ), jnp.float32)
        later = jnp.zeros((3, NY, NZ), jnp.float32)
        for a, (i, j, k) in enumerate(corners()):
            part = force[:, a, 1 - j:1 - j + NY, 1 - k:1 - k + NZ]
            if i == 0:
                here = here + part
            else:
                later = later + part
        return (later, carry + here)
    start = jnp.zeros((3, NY, NZ), jnp.float32)
    _, slabs = lax.scan(step, start, jnp.arange(NX, dtype=jnp.int32))
    return jnp.moveaxis(slabs, 0, 1)

def energy_global(first_field, second_field, stiffness):
    first_pad = jnp.pad(first_field, ((0, 0), (0, 1), (0, 1), (0, 1)))
    second_pad = jnp.pad(second_field, ((0, 0), (0, 1), (0, 1), (0, 1)))

    def step(carry, index):
        first_slab = lax.dynamic_slice_in_dim(first_pad, index, 2, 1)
        second_slab = lax.dynamic_slice_in_dim(second_pad, index, 2, 1)
        first_el = jnp.stack([first_slab[:, i, j:j + NY, k:k + NZ] for i, j, k in corners()], 1).reshape(24, NY * NZ)
        second_el = jnp.stack([second_slab[:, i, j:j + NY, k:k + NZ] for i, j, k in corners()], 1).reshape(24, NY * NZ)
        product = jnp.dot(stiffness, second_el, precision=lax.Precision.HIGHEST)
        return (carry, lax.optimization_barrier(jnp.sum(first_el * product, axis=0)).reshape(NY, NZ))
    _, slabs = lax.scan(step, jnp.zeros((), jnp.float32), jnp.arange(NX, dtype=jnp.int32))
    return slabs

def restrict(field):
    return field.reshape(3, NX // 2, 2, NY // 2, 2, NZ // 2, 2).sum(axis=(2, 4, 6))

def prolong(field):
    return jnp.repeat(jnp.repeat(jnp.repeat(field, 2, axis=1), 2, axis=2), 2, axis=3)

def reference(design, passive, fixed, state, adjoint, resid):
    table = element_matrix()
    stiffness = jnp.asarray(table, dtype=jnp.float32)
    stiff_diag = [[table[8 * c + a][8 * c + a] for a in range(8)] for c in range(3)]
    masked = jnp.where(passive == 1, 0.0, jnp.where(passive == 2, 1.0, design)).astype(jnp.float32)
    weight_sum = smooth(jnp.ones((NX, NY, NZ), jnp.float32))
    density = smooth(masked) / weight_sum
    factor = stiff_floor + density ** 3 * (1.0 - stiff_floor)
    free = (1 - fixed).astype(jnp.float32)
    factor_pad = jnp.pad(factor, ((1, 0), (1, 0), (1, 0)))
    rows = []
    for c in range(3):
        total = jnp.zeros((NX, NY, NZ), jnp.float32)
        for a, (i, j, k) in enumerate(corners()):
            total = total + float(stiff_diag[c][a]) * factor_pad[1 - i:1 - i + NX, 1 - j:1 - j + NY, 1 - k:1 - k + NZ]
        rows.append(total)
    diagonal = free * jnp.stack(rows, 0) + (1.0 - free)

    def operator(field):
        return free * apply_global(free * field, factor, stiffness) + (1.0 - free) * field
    first = damping * resid / diagonal
    second_res = resid - operator(first)
    coarse_res = restrict(second_res)
    coarse_diag = restrict(diagonal)
    coarse_first = coarse_damping * coarse_res / coarse_diag
    coarse_fix = coarse_first + coarse_damping * (coarse_res - restrict(operator(prolong(coarse_first)))) / coarse_diag
    middle = first + prolong(coarse_fix)
    direction = middle + damping * (resid - operator(middle)) / diagonal
    numerator = jnp.sum(resid * direction)
    image = operator(direction)
    denominator = jnp.sum(direction * image)
    step_size = numerator / denominator
    adjoint_new = adjoint + step_size * direction
    resid_new = resid - step_size * image
    energy = energy_global(adjoint_new, state, stiffness)
    sens = 3.0 * density ** 2 * (1.0 - stiff_floor) * energy
    grad = smooth(sens / weight_sum)
    design_grad = jnp.where(passive == 0, grad, 0.0).astype(jnp.float32)
    return (adjoint_new, resid_new, design_grad)
```

```python
import math

import jax
import jax.numpy as jnp
from jax import lax
from jax.experimental import pallas as pl
from jax.experimental.pallas import tpu as pltpu
from jax.sharding import PartitionSpec as P

stiff_floor = 0.001
damping = 0.6
coarse_damping = 0.5

MESH = pl.DeviceIdType.MESH
AXES = ("gx", "gy", "gz")
GROUPS = (24, 4, 8)
EDGE = 1.0
FACE = 2.0 - math.sqrt(2.0)
CORNER = 2.0 - math.sqrt(3.0)

LAME = 0.3 / (1.3 * 0.4)
SHEAR = 0.5 / 1.3
NORMAL = (LAME + 2.0 * SHEAR) / 16.0
CROSS = LAME / 16.0
TWIST = SHEAR / 16.0
BEND = (LAME + 2.0 * SHEAR + SHEAR) / 48.0
BEND_CROSS = LAME / 48.0
SPIN = SHEAR / 48.0
HOUR = (LAME + 2.0 * SHEAR + 2.0 * SHEAR) / 144.0
NODE_DIAG = (LAME + 2.0 * SHEAR + 2.0 * SHEAR) / 9.0

YZ = [(j, k) for j in (-1, 0, 1) for k in (-1, 0, 1) if (j, k) != (0, 0)]


def device(dx, dy, dz):
    return tuple(
        lax.rem(lax.axis_index(axis) + (step + count), count)
        for axis, step, count in zip(AXES, (dx, dy, dz), GROUPS)
    )


def partner():
    place = lax.axis_index("gx")
    return (place + 1 - 2 * lax.rem(place, 2), lax.axis_index("gy"), lax.axis_index("gz"))


def zp(v):
    return pltpu.roll(v, v.shape[1] - 1, 1)


def zm(v):
    return pltpu.roll(v, 1, 1)


def yp(v):
    return pltpu.roll(v, v.shape[0] - 1, 0)


def ym(v):
    return pltpu.roll(v, 1, 0)


def forward(field):
    modes = {}
    for c in range(3):
        u = field[c]
        up = zp(u)
        for r, w in ((0, u + up), (1, up - u)):
            wp = yp(w)
            modes[c, 0, r] = w + wp
            modes[c, 1, r] = wp - w
    return modes


def across(low, high):
    modes = {}
    for (c, q, r), a in low.items():
        b = high[c, q, r]
        if (q, r) != (0, 0):
            modes[c, 0, q, r] = a + b
        modes[c, 1, q, r] = b - a
    return modes


def stress(u):
    f = {}
    total = (u[0, 1, 0, 0] + u[1, 0, 1, 0] + u[2, 0, 0, 1]) * CROSS
    for c, mode in ((0, (1, 0, 0)), (1, (0, 1, 0)), (2, (0, 0, 1))):
        f[(c,) + mode] = u[(c,) + mode] * (NORMAL - CROSS) + total
    for a, b in (
        ((0, 0, 0, 1), (2, 1, 0, 0)),
        ((0, 0, 1, 0), (1, 1, 0, 0)),
        ((1, 0, 0, 1), (2, 0, 1, 0)),
    ):
        f[a] = f[b] = (u[a] + u[b]) * TWIST
    total = u[0, 0, 1, 1] + u[1, 1, 0, 1] + u[2, 1, 1, 0]
    for a in ((0, 0, 1, 1), (1, 1, 0, 1), (2, 1, 1, 0)):
        f[a] = (u[a] + total) * SPIN
    for a, b in (
        ((0, 1, 0, 1), (1, 0, 1, 1)),
        ((0, 1, 1, 0), (2, 0, 1, 1)),
        ((1, 1, 1, 0), (2, 1, 0, 1)),
    ):
        f[a] = u[a] * BEND + u[b] * BEND_CROSS
        f[b] = u[b] * BEND + u[a] * BEND_CROSS
    for c in range(3):
        f[c, 1, 1, 1] = u[c, 1, 1, 1] * HOUR
    return f


def scaled(f, factor):
    out, seen = {}, {}
    for mode, value in f.items():
        if id(value) not in seen:
            seen[id(value)] = value * factor
        out[mode] = seen[id(value)]
    return out


def backward(modes):
    rows = []
    for c in range(3):
        lines = []
        for r in (0, 1):
            s, d = modes[c, 0, r], modes[c, 1, r]
            lines.append((s - d) + ym(s + d))
        rows.append((lines[0] - lines[1]) + zm(lines[0] + lines[1]))
    return rows


def stiffness_product(nodes, factors):
    count = len(nodes)
    result, carry = [], None
    low = forward(nodes[0])
    for e in range(count - 1):
        high = forward(nodes[e + 1])
        f = scaled(stress(across(low, high)), factors[e])
        here, later = {}, {}
        for c, q, r in low:
            d = f[c, 1, q, r]
            if (q, r) == (0, 0):
                here[c, q, r] = -d
                later[c, q, r] = d
            else:
                s = f[c, 0, q, r]
                here[c, q, r] = s - d
                later[c, q, r] = s + d
        if carry is not None:
            result.append(backward({mode: carry[mode] + here[mode] for mode in here}))
        carry, low = later, high
    return result


def operator(planes, factors, free):
    held = [[free[p] * planes[p][c] for c in range(3)] for p in range(len(planes))]
    forces = stiffness_product(held, factors)
    return [
        [
            free[p] * forces[p - 1][c] + (planes[p][c] - held[p][c])
            for c in range(3)
        ]
        for p in range(1, len(planes) - 1)
    ]


def smooth_plane(v):
    along_z = zp(v) + zm(v)
    along_y = yp(v) + ym(v)
    both = yp(along_z) + ym(along_z)
    sides = along_z + along_y
    return 2.0 * v + EDGE * sides + FACE * both, EDGE * v + FACE * sides + CORNER * both


def smooth(planes):
    parts = [smooth_plane(v) for v in planes]
    return [
        parts[p][0] + (parts[p - 1][1] + parts[p + 1][1]) for p in range(1, len(planes) - 1)
    ]


def block_sum(low, high, even_y, even_z):
    v = low + high
    v = v + jnp.where(even_z, zp(v), zm(v))
    return v + jnp.where(even_y, yp(v), ym(v))


def iota(shape, dim):
    return lax.broadcasted_iota(jnp.int32, shape, dim)


def pack(tiles):
    slot = iota((8, 128), 1) >> 3
    packs = []
    for first in range(0, len(tiles), 16):
        total = None
        for s, tile in enumerate(tiles[first : first + 16]):
            turned = pltpu.roll(tile, (4 + 8 * s) % 128, 1)
            total = turned if total is None else jnp.where(slot == s, turned, total)
        packs.append(total)
    return packs


def unpack(packed, s):
    return pltpu.roll(packed, (124 - 8 * (s % 16)) % 128, 1)


def kernel(
    design_hbm, passive_hbm, fixed_hbm, state_hbm, adjoint_hbm, resid_hbm,
    adjoint_out, resid_out, grad_out,
    design, passive, fixed, own_sa, in_sem,
    own0, z0, ly0, lz0, lc0, em0, er0, ea0, xm0, xf0, xr0, xa0,
    z2, ly2, lz2, lc2, e2, x2,
    own1, z1, ly1, lz1, lc1, e1, x1,
    own3, z3, ly3, lz3, lc3, e3, x3,
    ar_send, ar_land, send_sem, recv_sem,
):
    copies = []

    def send(src, dst, target):
        number = len(copies)
        copy = pltpu.make_async_remote_copy(
            src_ref=src,
            dst_ref=dst,
            send_sem=send_sem.at[number],
            recv_sem=recv_sem.at[number],
            device_id=target,
            device_id_type=MESH,
        )
        copy.start()
        copies.append(copy)
        return copy

    def arrive(group):
        for copy in group:
            copy.wait_recv()

    barrier = pltpu.get_barrier_semaphore()
    friends = [(0, j, k) for j, k in YZ] + [(1, 0, 0), (-1, 0, 0)]
    friends += [(2 * i, 0, 0) for i in range(1, 12)] + [(0, 2, 0)] + [(0, 0, k) for k in range(2, 7)]
    for friend in friends:
        pl.semaphore_signal(barrier, inc=1, device_id=device(*friend), device_id_type=MESH)

    inputs = [
        pltpu.make_async_copy(src, dst, in_sem.at[n])
        for n, (src, dst) in enumerate(
            (
                (design_hbm, design),
                (passive_hbm, passive),
                (fixed_hbm, fixed),
                (resid_hbm, own0.at[pl.ds(8, 12)]),
                (adjoint_hbm, own_sa.at[pl.ds(0, 12)]),
                (state_hbm, own_sa.at[pl.ds(12, 12)]),
            )
        )
    ]
    for copy in inputs:
        copy.start()

    place_x, place_y, place_z = (lax.axis_index(axis) for axis in AXES)
    wide = (16, 256)
    row, lane = iota(wide, 0), iota(wide, 1)
    at_y = place_y * 8 + jnp.where(row < 12, row, row - 16)
    at_z = place_z * 128 + jnp.where(lane < 192, lane, lane - 256)
    inside = ((at_y >= 0) & (at_y < 32) & (at_z >= 0) & (at_z < 1024)).astype(jnp.float32)
    inside_low = inside * (place_x > 0).astype(jnp.float32)
    inside_high = inside * (place_x < 23).astype(jnp.float32)

    def sides(dim_at, count):
        return (dim_at > 0).astype(jnp.float32) + (dim_at < count - 1).astype(jnp.float32)

    near_y, near_z = sides(at_y, 32), sides(at_z, 1024)
    near, nearer = near_y + near_z, near_y * near_z
    weight_base = 2.0 + EDGE * near + FACE * nearer
    weight_step = EDGE + FACE * near + CORNER * nearer
    inverse_inner = 1.0 / (weight_base + 2.0 * weight_step)
    inverse_end = 1.0 / (weight_base + weight_step)
    inverse_first = jnp.where(place_x > 0, inverse_inner, inverse_end)
    inverse_last = jnp.where(place_x < 23, inverse_inner, inverse_end)

    def inverse_weight(p):
        return inverse_first if p == 0 else inverse_last if p == 3 else inverse_inner

    even_y, even_z = (row & 1) == 0, (lane & 1) == 0
    tile_even_y, tile_even_z = (iota((8, 128), 0) & 1) == 0, (iota((8, 128), 1) & 1) == 0
    top_half = iota((8, 128), 0) < 4
    low_slot = (iota((8, 128), 1) & 7) < 4

    for copy in inputs[:3]:
        copy.wait()
    own0[0:4] = jnp.where(passive[...] == 1, 0.0, jnp.where(passive[...] == 2, 1.0, design[...]))
    own0[4:8] = (1 - fixed[...]).astype(jnp.float32)
    inputs[3].wait()
    for n, packed in enumerate(pack([own0[t] for t in range(20)])):
        z0[n] = packed
    pl.semaphore_wait(barrier, len(friends))

    def flat_sends(own, edges, land_y, land_z, land_c):
        group = {}
        for n, (j, k) in enumerate((j, k) for j in (-1, 1) for k in (-1, 1)):
            group[j, k] = send(edges, land_c.at[n], device(0, j, k))
        for n, k in enumerate((-1, 1)):
            group[0, k] = send(edges, land_z.at[n], device(0, 0, k))
        for n, j in enumerate((-1, 1)):
            group[j, 0] = send(own, land_y.at[n], device(0, j, 0))
        return group.values()

    def rows_beside(land_y, t):
        return jnp.where(top_half, land_y[0, t], land_y[1, t])

    def edges_beside(land_z, land_c, n):
        top = jnp.where(low_slot, land_z[1, n], land_z[0, n])
        from_low_y = jnp.where(low_slot, land_c[3, n], land_c[2, n])
        from_high_y = jnp.where(low_slot, land_c[1, n], land_c[0, n])
        return jnp.concatenate([top, jnp.where(top_half, from_high_y, from_low_y)], 0)

    def widened(main, packed, s):
        return jnp.concatenate([main, unpack(packed, s)], 1)

    arrive(flat_sends(own0, z0, ly0, lz0, lc0))
    edges0 = [edges_beside(lz0, lc0, n) for n in range(2)]
    mains = [jnp.concatenate([own0[t], rows_beside(ly0, t)], 0) for t in range(20)]
    for t in range(8):
        em0[t] = mains[t]
    for t in range(12):
        er0[t // 4, t % 4] = mains[8 + t]
    for n in range(2):
        ea0[n] = edges0[n]
    group = [
        send(em0.at[pl.ds(0, 3)], xm0.at[0, pl.ds(0, 3)], device(-1, 0, 0)),
        send(em0.at[pl.ds(4, 3)], xf0.at[0], device(-1, 0, 0)),
        send(er0.at[:, pl.ds(0, 2)], xr0.at[0], device(-1, 0, 0)),
        send(ea0, xa0.at[0], device(-1, 0, 0)),
        send(em0.at[pl.ds(0, 4)], xm0.at[1], device(1, 0, 0)),
        send(em0.at[pl.ds(5, 3)], xf0.at[1], device(1, 0, 0)),
        send(er0.at[:, pl.ds(2, 2)], xr0.at[1], device(1, 0, 0)),
        send(ea0, xa0.at[1], device(1, 0, 0)),
    ]

    inputs[4].wait()
    inputs[5].wait()
    for n, packed in enumerate(pack([own_sa[t] for t in range(24)])):
        z2[n] = packed
    group2 = [
        send(own_sa, ly2, device(0, -1, 0)),
        send(z2, lz2, device(0, 0, -1)),
        send(z2, lc2, device(0, -1, -1)),
    ]

    arrive(group)
    masked = [widened(xm0[1, p], xa0[1, 0], p) * inside_low for p in range(4)]
    masked += [widened(mains[p], edges0[0], p) * inside for p in range(4)]
    masked += [widened(xm0[0, p], xa0[0, 0], p) * inside_high for p in range(3)]
    free = [widened(xf0[1, p], xa0[1, 0], 5 + p) * inside_low for p in range(3)]
    free += [widened(mains[4 + p], edges0[0], 4 + p) * inside for p in range(4)]
    free += [widened(xf0[0, p], xa0[0, 0], 4 + p) * inside_high for p in range(3)]
    resid = [
        [widened(xr0[1, c, p], xa0[1, (10 + 4 * c + p) // 16], 10 + 4 * c + p) * inside_low for c in range(3)]
        for p in range(2)
    ]
    resid += [
        [widened(mains[8 + 4 * c + p], edges0[(8 + 4 * c + p) // 16], 8 + 4 * c + p) * inside for c in range(3)]
        for p in range(4)
    ]
    resid += [
        [widened(xr0[0, c, p], xa0[0, (8 + 4 * c + p) // 16], 8 + 4 * c + p) * inside_high for c in range(3)]
        for p in range(2)
    ]

    smoothed = smooth(masked)
    density, factor = {}, {}
    for p in range(-3, 6):
        inverse = inverse_weight(p) if 0 <= p < 4 else inverse_inner
        if p == -1 or p == 4:
            inverse = inverse_inner
        if p == -3:
            inverse = inverse_inner
        density[p] = smoothed[p + 3] * inverse
    for p in range(-3, 6):
        edge = inside_low if p < 0 else inside if p < 4 else inside_high
        d = density[p]
        factor[p] = edge * (stiff_floor + d * d * d * (1.0 - stiff_floor))

    paired = {}
    for p in range(-3, 6):
        v = factor[p] + zm(factor[p])
        paired[p] = v + ym(v)
    free = {p: free[p + 3] for p in range(-3, 7)}
    resid = {p: resid[p + 2] for p in range(-2, 6)}
    diagonal, inverse_diag, first = {}, {}, {}
    for p in range(-2, 6):
        diagonal[p] = free[p] * (NODE_DIAG * (paired[p] + paired[p - 1])) + (1.0 - free[p])
        inverse_diag[p] = 1.0 / diagonal[p]
        first[p] = [damping * resid[p][c] * inverse_diag[p] for c in range(3)]

    def apply(field, lowest, highest):
        span = range(lowest - 1, highest + 2)
        result = operator(
            [field[p] for p in span],
            [factor[p] for p in range(lowest - 1, highest + 1)],
            [free[p] for p in span],
        )
        return {p: result[p - lowest] for p in range(lowest, highest + 1)}

    image = apply(first, 0, 3)
    second = [
        [(resid[p][c] - image[p][c])[0:8, 0:128] for c in range(3)] for p in range(4)
    ]
    coarse_diag = [
        block_sum(diagonal[2 * k], diagonal[2 * k + 1], even_y, even_z) for k in range(-1, 3)
    ]
    inverse_coarse = [1.0 / d for d in coarse_diag]
    coarse_own = []
    for c in range(3):
        for k in range(2):
            total = block_sum(second[2 * k][c], second[2 * k + 1][c], tile_even_y, tile_even_z)
            coarse_own.append(coarse_damping * total * inverse_coarse[k + 1][0:8, 0:128])
    for t in range(6):
        own1[t] = coarse_own[t]
    z1[0] = pack(coarse_own)[0]
    group = flat_sends(own1, z1, ly1, lz1, lc1)

    arrive(group2)
    edges2 = []
    for n in range(2):
        edges2.append(jnp.concatenate([lz2[n], lc2[n]], 0))
        e2[6 + n] = edges2[n]
    mains2 = [jnp.concatenate([own_sa[t], ly2[t]], 0) for t in range(24)]
    for f in range(6):
        e2[f] = mains2[4 * f]

    arrive(group)
    edges1 = edges_beside(lz1, lc1, 0)
    mains1 = [jnp.concatenate([coarse_own[t], rows_beside(ly1, t)], 0) for t in range(6)]
    for t in range(6):
        e1[t] = mains1[t]
    e1[6] = edges1
    group = [
        send(e1, x1.at[0], device(-1, 0, 0)),
        send(e1, x1.at[1], device(1, 0, 0)),
    ]
    group2 = [send(e2, x2, device(-1, 0, 0))]
    arrive(group)
    coarse = {}
    for k in range(2):
        coarse[k - 2] = [widened(x1[1, 2 * c + k], x1[1, 6], 2 * c + k) * inside_low for c in range(3)]
        coarse[k] = [widened(mains1[2 * c + k], edges1, 2 * c + k) * inside for c in range(3)]
        coarse[k + 2] = [widened(x1[0, 2 * c + k], x1[0, 6], 2 * c + k) * inside_high for c in range(3)]
    spread = {p: coarse[p // 2] for p in range(-4, 8)}
    image = apply(spread, -2, 5)
    middle = {}
    for k in range(-1, 3):
        for c in range(3):
            total = block_sum(image[2 * k][c], image[2 * k + 1][c], even_y, even_z)
            fix = 2.0 * coarse[k][c] - coarse_damping * total * inverse_coarse[k + 1]
            for p in (2 * k, 2 * k + 1):
                middle.setdefault(p, []).append(first[p][c] + fix)
    image = apply(middle, -1, 4)
    direction = {
        p: [
            middle[p][c] + damping * (resid[p][c] - image[p][c]) * inverse_diag[p]
            for c in range(3)
        ]
        for p in range(-1, 5)
    }
    image = apply(direction, 0, 3)
    image = {p: [image[p][c][0:8, 0:128] for c in range(3)] for p in range(4)}
    numerator = denominator = None
    for p in range(4):
        for c in range(3):
            d = direction[p][c][0:8, 0:128]
            a, b = resid[p][c][0:8, 0:128] * d, d * image[p][c]
            numerator = a if numerator is None else numerator + a
            denominator = b if denominator is None else denominator + b
    numerator = numerator + pltpu.roll(numerator, 4, 0)
    denominator = denominator + pltpu.roll(denominator, 4, 0)
    sums = jnp.where(top_half, numerator, denominator)

    landed = [0]

    def spread_sums(stage, value, targets):
        ar_send[stage] = value
        base = landed[0]
        landed[0] += len(targets)
        group = [
            send(ar_send.at[stage], ar_land.at[base + n], target)
            for n, target in enumerate(targets)
        ]

        def gather():
            arrive(group)
            total = value
            for n in range(len(targets)):
                total = total + ar_land[base + n]
            return total

        return gather

    sums = spread_sums(0, sums, [partner()])()
    gather = spread_sums(1, sums, [device(2 * i, 0, 0) for i in (6, 5, 7, 4, 8, 3, 9, 2, 10, 1, 11)])

    arrive(group2)
    def ends(f, p):
        if p < 4:
            return widened(mains2[4 * f + p], edges2[(4 * f + p) // 16], 4 * f + p) * inside
        return widened(x2[f], x2[6 + (4 * f) // 16], 4 * f) * inside_high

    def corner_modes(fields):
        return [{m: v[0:8, 0:128] for m, v in forward(fields[p]).items()} for p in range(5)]

    adjoint_modes = corner_modes([[ends(c, p) for c in range(3)] for p in range(5)])
    state_modes = corner_modes([[ends(3 + c, p) for c in range(3)] for p in range(5)])
    direction_modes = corner_modes([direction[p] for p in range(5)])
    sens = []
    for p in range(4):
        force = stress(across(state_modes[p], state_modes[p + 1]))
        d = density[p][0:8, 0:128]
        weight = 3.0 * (1.0 - stiff_floor) * d * d * inverse_weight(p)[0:8, 0:128]
        for modes in (adjoint_modes, direction_modes):
            with_modes = across(modes[p], modes[p + 1])
            energy = None
            for mode, value in force.items():
                term = with_modes[mode] * value
                energy = term if energy is None else energy + term
            sens.append(weight * energy)
    for t in range(8):
        own3[t] = sens[t]
    z3[0] = pack(sens)[0]
    group = flat_sends(own3, z3, ly3, lz3, lc3)
    sums = gather()
    gather = spread_sums(2, sums, [device(0, 0, k) for k in (4, 3, 5, 2, 6, 1, 7)])
    arrive(group)
    edges3 = edges_beside(lz3, lc3, 0)
    mains3 = [jnp.concatenate([sens[t], rows_beside(ly3, t)], 0) for t in range(8)]
    e3[0] = mains3[0]
    e3[1] = mains3[1]
    e3[2] = edges3
    e3[3] = mains3[6]
    e3[4] = mains3[7]
    group = [
        send(e3.at[pl.ds(0, 3)], x3.at[0], device(-1, 0, 0)),
        send(e3.at[pl.ds(2, 3)], x3.at[1], device(1, 0, 0)),
    ]
    sums = gather()
    gather = spread_sums(3, sums, [device(0, j, 0) for j in (2, 1, 3)])
    arrive(group)
    grads = []
    for f in range(2):
        planes = [widened(x3[1, 1 + f], x3[1, 0], 6 + f) * inside_low]
        planes += [widened(mains3[2 * p + f], edges3, 2 * p + f) * inside for p in range(4)]
        planes += [widened(x3[0, f], x3[0, 2], f) * inside_high]
        grads.append([v[0:8, 0:128] for v in smooth(planes)])
    sums = gather()
    numerator = jnp.sum(jnp.where(top_half, sums, 0.0), axis=(0, 1), keepdims=True)
    denominator = jnp.sum(jnp.where(top_half, 0.0, sums), axis=(0, 1), keepdims=True)
    step = jnp.broadcast_to(numerator / denominator, (8, 128))
    for p in range(4):
        for c in range(3):
            adjoint_out[c, p] = own_sa[4 * c + p] + step * direction[p][c][0:8, 0:128]
            resid_out[c, p] = own0[8 + 4 * c + p] - step * image[p][c]
        grad_out[p] = jnp.where(passive[p] == 0, grads[0][p] + step * grads[1][p], 0.0)
    for copy in copies:
        copy.wait_send()


def body(design, passive, fixed, state, adjoint, resid):
    def scratch(*shape):
        return pltpu.VMEM(shape, jnp.float32)

    n_copies = 8 + 8 + 3 + 8 + 2 + 1 + 22 + 8 + 2
    return pl.pallas_call(
        kernel,
        out_shape=(
            jax.ShapeDtypeStruct((3, 4, 8, 128), jnp.float32),
            jax.ShapeDtypeStruct((3, 4, 8, 128), jnp.float32),
            jax.ShapeDtypeStruct((4, 8, 128), jnp.float32),
        ),
        in_specs=[pl.BlockSpec(memory_space=pl.ANY)] * 6,
        out_specs=(pl.BlockSpec(memory_space=pltpu.VMEM),) * 3,
        scratch_shapes=[
            scratch(4, 8, 128),
            pltpu.VMEM((4, 8, 128), jnp.int32),
            pltpu.VMEM((4, 8, 128), jnp.int32),
            scratch(24, 8, 128),
            pltpu.SemaphoreType.DMA((6,)),
            scratch(20, 8, 128),
            scratch(2, 8, 128),
            scratch(2, 20, 8, 128),
            scratch(2, 2, 8, 128),
            scratch(4, 2, 8, 128),
            scratch(8, 16, 128),
            scratch(3, 4, 16, 128),
            scratch(2, 16, 128),
            scratch(2, 4, 16, 128),
            scratch(2, 3, 16, 128),
            scratch(2, 3, 2, 16, 128),
            scratch(2, 2, 16, 128),
            scratch(2, 8, 128),
            scratch(24, 8, 128),
            scratch(2, 8, 128),
            scratch(2, 8, 128),
            scratch(8, 16, 128),
            scratch(8, 16, 128),
            scratch(6, 8, 128),
            scratch(1, 8, 128),
            scratch(2, 6, 8, 128),
            scratch(2, 1, 8, 128),
            scratch(4, 1, 8, 128),
            scratch(7, 16, 128),
            scratch(2, 7, 16, 128),
            scratch(8, 8, 128),
            scratch(1, 8, 128),
            scratch(2, 8, 8, 128),
            scratch(2, 1, 8, 128),
            scratch(4, 1, 8, 128),
            scratch(5, 16, 128),
            scratch(2, 3, 16, 128),
            scratch(4, 8, 128),
            scratch(22, 8, 128),
            pltpu.SemaphoreType.DMA((n_copies,)),
            pltpu.SemaphoreType.DMA((n_copies,)),
        ],
        compiler_params=pltpu.CompilerParams(
            collective_id=0, has_side_effects=True, vmem_limit_bytes=32 * 2**20
        ),
    )(
        design,
        passive,
        fixed,
        state.reshape(12, 8, 128),
        adjoint.reshape(12, 8, 128),
        resid.reshape(12, 8, 128),
    )


def solution(mesh):
    return jax.shard_map(
        body,
        mesh=mesh,
        in_specs=(P("gx", "gy", "gz"),) * 3 + (P(None, "gx", "gy", "gz"),) * 3,
        out_specs=(P(None, "gx", "gy", "gz"), P(None, "gx", "gy", "gz"), P("gx", "gy", "gz")),
        check_vma=False,
    )
```

```python
import math

import jax
import jax.numpy as jnp
from jax import lax
from jax.experimental import pallas as pl
from jax.experimental.pallas import tpu as pltpu
from jax.sharding import PartitionSpec as P

stiff_floor = 0.001
damping = 0.6
coarse_damping = 0.5

MESH = pl.DeviceIdType.MESH
AXES = ("gx", "gy", "gz")
GROUPS = (24, 4, 8)
EDGE = 1.0
FACE = 2.0 - math.sqrt(2.0)
CORNER = 2.0 - math.sqrt(3.0)

LAME = 0.3 / (1.3 * 0.4)
SHEAR = 0.5 / 1.3
NORMAL = (LAME + 2.0 * SHEAR) / 16.0
CROSS = LAME / 16.0
TWIST = SHEAR / 16.0
BEND = (LAME + 2.0 * SHEAR + SHEAR) / 48.0
BEND_CROSS = LAME / 48.0
SPIN = SHEAR / 48.0
HOUR = (LAME + 2.0 * SHEAR + 2.0 * SHEAR) / 144.0
NODE_DIAG = (LAME + 2.0 * SHEAR + 2.0 * SHEAR) / 9.0

YZ = [(j, k) for j in (-1, 0, 1) for k in (-1, 0, 1) if (j, k) != (0, 0)]


def device(dx, dy, dz):
    return tuple(
        lax.rem(lax.axis_index(axis) + (step + count), count)
        for axis, step, count in zip(AXES, (dx, dy, dz), GROUPS)
    )


def partner():
    place = lax.axis_index("gx")
    return (place + 1 - 2 * lax.rem(place, 2), lax.axis_index("gy"), lax.axis_index("gz"))


def zp(v):
    return pltpu.roll(v, v.shape[1] - 1, 1)


def zm(v):
    return pltpu.roll(v, 1, 1)


def yp(v):
    return pltpu.roll(v, v.shape[0] - 1, 0)


def ym(v):
    return pltpu.roll(v, 1, 0)


def forward(field):
    modes = {}
    for c in range(3):
        u = field[c]
        up = zp(u)
        for r, w in ((0, u + up), (1, up - u)):
            wp = yp(w)
            modes[c, 0, r] = w + wp
            modes[c, 1, r] = wp - w
    return modes


def across(low, high):
    modes = {}
    for (c, q, r), a in low.items():
        b = high[c, q, r]
        if (q, r) != (0, 0):
            modes[c, 0, q, r] = a + b
        modes[c, 1, q, r] = b - a
    return modes


def stress(u):
    f = {}
    total = (u[0, 1, 0, 0] + u[1, 0, 1, 0] + u[2, 0, 0, 1]) * CROSS
    for c, mode in ((0, (1, 0, 0)), (1, (0, 1, 0)), (2, (0, 0, 1))):
        f[(c,) + mode] = u[(c,) + mode] * (NORMAL - CROSS) + total
    for a, b in (
        ((0, 0, 0, 1), (2, 1, 0, 0)),
        ((0, 0, 1, 0), (1, 1, 0, 0)),
        ((1, 0, 0, 1), (2, 0, 1, 0)),
    ):
        f[a] = f[b] = (u[a] + u[b]) * TWIST
    total = u[0, 0, 1, 1] + u[1, 1, 0, 1] + u[2, 1, 1, 0]
    for a in ((0, 0, 1, 1), (1, 1, 0, 1), (2, 1, 1, 0)):
        f[a] = (u[a] + total) * SPIN
    for a, b in (
        ((0, 1, 0, 1), (1, 0, 1, 1)),
        ((0, 1, 1, 0), (2, 0, 1, 1)),
        ((1, 1, 1, 0), (2, 1, 0, 1)),
    ):
        f[a] = u[a] * BEND + u[b] * BEND_CROSS
        f[b] = u[b] * BEND + u[a] * BEND_CROSS
    for c in range(3):
        f[c, 1, 1, 1] = u[c, 1, 1, 1] * HOUR
    return f


def scaled(f, factor):
    out, seen = {}, {}
    for mode, value in f.items():
        if id(value) not in seen:
            seen[id(value)] = value * factor
        out[mode] = seen[id(value)]
    return out


def backward(modes):
    rows = []
    for c in range(3):
        lines = []
        for r in (0, 1):
            s, d = modes[c, 0, r], modes[c, 1, r]
            lines.append((s - d) + ym(s + d))
        rows.append((lines[0] - lines[1]) + zm(lines[0] + lines[1]))
    return rows


def stiffness_product(nodes, factors):
    count = len(nodes)
    result, carry = [], None
    low = forward(nodes[0])
    for e in range(count - 1):
        high = forward(nodes[e + 1])
        f = scaled(stress(across(low, high)), factors[e])
        here, later = {}, {}
        for c, q, r in low:
            d = f[c, 1, q, r]
            if (q, r) == (0, 0):
                here[c, q, r] = -d
                later[c, q, r] = d
            else:
                s = f[c, 0, q, r]
                here[c, q, r] = s - d
                later[c, q, r] = s + d
        if carry is not None:
            result.append(backward({mode: carry[mode] + here[mode] for mode in here}))
        carry, low = later, high
    return result


def operator(planes, factors, free):
    held = [[free[p] * planes[p][c] for c in range(3)] for p in range(len(planes))]
    forces = stiffness_product(held, factors)
    return [
        [
            free[p] * forces[p - 1][c] + (planes[p][c] - held[p][c])
            for c in range(3)
        ]
        for p in range(1, len(planes) - 1)
    ]


def smooth_plane(v):
    along_z = zp(v) + zm(v)
    along_y = yp(v) + ym(v)
    both = yp(along_z) + ym(along_z)
    sides = along_z + along_y
    return 2.0 * v + EDGE * sides + FACE * both, EDGE * v + FACE * sides + CORNER * both


def smooth(planes):
    parts = [smooth_plane(v) for v in planes]
    return [
        parts[p][0] + (parts[p - 1][1] + parts[p + 1][1]) for p in range(1, len(planes) - 1)
    ]


def block_sum(low, high, even_y, even_z):
    v = low + high
    v = v + jnp.where(even_z, zp(v), zm(v))
    return v + jnp.where(even_y, yp(v), ym(v))


def iota(shape, dim):
    return lax.broadcasted_iota(jnp.int32, shape, dim)


def pack(tiles):
    slot = iota((8, 128), 1) >> 3
    packs = []
    for first in range(0, len(tiles), 16):
        total = None
        for s, tile in enumerate(tiles[first : first + 16]):
            turned = pltpu.roll(tile, (4 + 8 * s) % 128, 1)
            total = turned if total is None else jnp.where(slot == s, turned, total)
        packs.append(total)
    return packs


def unpack(packed, s):
    return pltpu.roll(packed, (124 - 8 * (s % 16)) % 128, 1)


def kernel(
    design_hbm, passive_hbm, fixed_hbm, state_hbm, adjoint_hbm, resid_hbm,
    adjoint_out, resid_out, grad_out,
    design, passive, fixed, own_sa, in_sem,
    own0, z0, ly0, lz0, lc0, em0, er0, ea0, xm0, xf0, xr0, xa0,
    z2, ly2, lz2, lc2, e2, x2,
    own1, z1, ly1, lz1, lc1, e1, x1,
    own3, z3, ly3, lz3, lc3, e3, x3,
    ar_send, ar_land, send_sem, recv_sem,
):
    copies = []

    def send(src, dst, target):
        number = len(copies)
        copy = pltpu.make_async_remote_copy(
            src_ref=src,
            dst_ref=dst,
            send_sem=send_sem.at[number],
            recv_sem=recv_sem.at[number],
            device_id=target,
            device_id_type=MESH,
        )
        copy.start()
        copies.append(copy)
        return copy

    def arrive(group):
        for copy in group:
            copy.wait_recv()

    barrier = pltpu.get_barrier_semaphore()
    friends = [(0, j, k) for j, k in YZ] + [(1, 0, 0), (-1, 0, 0)]
    friends += [(2 * i, 0, 0) for i in (1, -1, 2, -2)]
    for friend in friends:
        pl.semaphore_signal(barrier, inc=1, device_id=device(*friend), device_id_type=MESH)

    inputs = [
        pltpu.make_async_copy(src, dst, in_sem.at[n])
        for n, (src, dst) in enumerate(
            (
                (design_hbm, design),
                (passive_hbm, passive),
                (fixed_hbm, fixed),
                (resid_hbm, own0.at[pl.ds(8, 12)]),
                (adjoint_hbm, own_sa.at[pl.ds(0, 12)]),
                (state_hbm, own_sa.at[pl.ds(12, 12)]),
            )
        )
    ]
    for copy in inputs:
        copy.start()

    place_x, place_y, place_z = (lax.axis_index(axis) for axis in AXES)
    wide = (16, 256)
    row, lane = iota(wide, 0), iota(wide, 1)
    at_y = place_y * 8 + jnp.where(row < 12, row, row - 16)
    at_z = place_z * 128 + jnp.where(lane < 192, lane, lane - 256)
    inside = ((at_y >= 0) & (at_y < 32) & (at_z >= 0) & (at_z < 1024)).astype(jnp.float32)
    inside_low = inside * (place_x > 0).astype(jnp.float32)
    inside_high = inside * (place_x < 23).astype(jnp.float32)

    def sides(dim_at, count):
        return (dim_at > 0).astype(jnp.float32) + (dim_at < count - 1).astype(jnp.float32)

    near_y, near_z = sides(at_y, 32), sides(at_z, 1024)
    near, nearer = near_y + near_z, near_y * near_z
    weight_base = 2.0 + EDGE * near + FACE * nearer
    weight_step = EDGE + FACE * near + CORNER * nearer
    inverse_inner = 1.0 / (weight_base + 2.0 * weight_step)
    inverse_end = 1.0 / (weight_base + weight_step)
    inverse_first = jnp.where(place_x > 0, inverse_inner, inverse_end)
    inverse_last = jnp.where(place_x < 23, inverse_inner, inverse_end)

    def inverse_weight(p):
        return inverse_first if p == 0 else inverse_last if p == 3 else inverse_inner

    even_y, even_z = (row & 1) == 0, (lane & 1) == 0
    tile_even_y, tile_even_z = (iota((8, 128), 0) & 1) == 0, (iota((8, 128), 1) & 1) == 0
    top_half = iota((8, 128), 0) < 4
    low_slot = (iota((8, 128), 1) & 7) < 4

    for copy in inputs[:3]:
        copy.wait()
    own0[0:4] = jnp.where(passive[...] == 1, 0.0, jnp.where(passive[...] == 2, 1.0, design[...]))
    own0[4:8] = (1 - fixed[...]).astype(jnp.float32)
    inputs[3].wait()
    for n, packed in enumerate(pack([own0[t] for t in range(20)])):
        z0[n] = packed
    pl.semaphore_wait(barrier, len(friends))

    def flat_sends(own, edges, land_y, land_z, land_c):
        group = {}
        for n, (j, k) in enumerate((j, k) for j in (-1, 1) for k in (-1, 1)):
            group[j, k] = send(edges, land_c.at[n], device(0, j, k))
        for n, k in enumerate((-1, 1)):
            group[0, k] = send(edges, land_z.at[n], device(0, 0, k))
        for n, j in enumerate((-1, 1)):
            half = pl.ds(4 * n, 4)
            group[j, 0] = send(own.at[:, half], land_y.at[:, half], device(0, j, 0))
        return group.values()

    def rows_beside(land_y, t):
        return land_y[t]

    def edges_beside(land_z, land_c, n):
        top = jnp.where(low_slot, land_z[1, n], land_z[0, n])
        from_low_y = jnp.where(low_slot, land_c[3, n], land_c[2, n])
        from_high_y = jnp.where(low_slot, land_c[1, n], land_c[0, n])
        return jnp.concatenate([top, jnp.where(top_half, from_high_y, from_low_y)], 0)

    def widened(main, packed, s):
        return jnp.concatenate([main, unpack(packed, s)], 1)

    arrive(flat_sends(own0, z0, ly0, lz0, lc0))
    edges0 = [edges_beside(lz0, lc0, n) for n in range(2)]
    mains = [jnp.concatenate([own0[t], rows_beside(ly0, t)], 0) for t in range(20)]
    for t in range(8):
        em0[t] = mains[t]
    for t in range(12):
        er0[t // 4, t % 4] = mains[8 + t]
    for n in range(2):
        ea0[n] = edges0[n]
    group = [
        send(em0.at[pl.ds(0, 3)], xm0.at[0, pl.ds(0, 3)], device(-1, 0, 0)),
        send(em0.at[pl.ds(4, 3)], xf0.at[0], device(-1, 0, 0)),
        send(er0.at[:, pl.ds(0, 2)], xr0.at[0], device(-1, 0, 0)),
        send(ea0, xa0.at[0], device(-1, 0, 0)),
        send(em0.at[pl.ds(0, 4)], xm0.at[1], device(1, 0, 0)),
        send(em0.at[pl.ds(5, 3)], xf0.at[1], device(1, 0, 0)),
        send(er0.at[:, pl.ds(2, 2)], xr0.at[1], device(1, 0, 0)),
        send(ea0, xa0.at[1], device(1, 0, 0)),
    ]

    inputs[4].wait()
    inputs[5].wait()
    for n, packed in enumerate(pack([own_sa[t] for t in range(24)])):
        z2[n] = packed
    group2 = [
        send(own_sa.at[:, pl.ds(0, 1)], ly2.at[:, pl.ds(0, 1)], device(0, -1, 0)),
        send(z2, lz2, device(0, 0, -1)),
        send(z2, lc2, device(0, -1, -1)),
    ]

    arrive(group)
    masked = [widened(xm0[1, p], xa0[1, 0], p) * inside_low for p in range(4)]
    masked += [widened(mains[p], edges0[0], p) * inside for p in range(4)]
    masked += [widened(xm0[0, p], xa0[0, 0], p) * inside_high for p in range(3)]
    free = [widened(xf0[1, p], xa0[1, 0], 5 + p) * inside_low for p in range(3)]
    free += [widened(mains[4 + p], edges0[0], 4 + p) * inside for p in range(4)]
    free += [widened(xf0[0, p], xa0[0, 0], 4 + p) * inside_high for p in range(3)]
    resid = [
        [widened(xr0[1, c, p], xa0[1, (10 + 4 * c + p) // 16], 10 + 4 * c + p) * inside_low for c in range(3)]
        for p in range(2)
    ]
    resid += [
        [widened(mains[8 + 4 * c + p], edges0[(8 + 4 * c + p) // 16], 8 + 4 * c + p) * inside for c in range(3)]
        for p in range(4)
    ]
    resid += [
        [widened(xr0[0, c, p], xa0[0, (8 + 4 * c + p) // 16], 8 + 4 * c + p) * inside_high for c in range(3)]
        for p in range(2)
    ]

    smoothed = smooth(masked)
    density, factor = {}, {}
    for p in range(-3, 6):
        inverse = inverse_weight(p) if 0 <= p < 4 else inverse_inner
        if p == -1 or p == 4:
            inverse = inverse_inner
        if p == -3:
            inverse = inverse_inner
        density[p] = smoothed[p + 3] * inverse
    for p in range(-3, 6):
        edge = inside_low if p < 0 else inside if p < 4 else inside_high
        d = density[p]
        factor[p] = edge * (stiff_floor + d * d * d * (1.0 - stiff_floor))

    paired = {}
    for p in range(-3, 6):
        v = factor[p] + zm(factor[p])
        paired[p] = v + ym(v)
    free = {p: free[p + 3] for p in range(-3, 7)}
    resid = {p: resid[p + 2] for p in range(-2, 6)}
    diagonal, inverse_diag, first = {}, {}, {}
    for p in range(-2, 6):
        diagonal[p] = free[p] * (NODE_DIAG * (paired[p] + paired[p - 1])) + (1.0 - free[p])
        inverse_diag[p] = 1.0 / diagonal[p]
        first[p] = [damping * resid[p][c] * inverse_diag[p] for c in range(3)]

    def apply(field, lowest, highest):
        span = range(lowest - 1, highest + 2)
        result = operator(
            [field[p] for p in span],
            [factor[p] for p in range(lowest - 1, highest + 1)],
            [free[p] for p in span],
        )
        return {p: result[p - lowest] for p in range(lowest, highest + 1)}

    image = apply(first, 0, 3)
    second = [
        [(resid[p][c] - image[p][c])[0:8, 0:128] for c in range(3)] for p in range(4)
    ]
    coarse_diag = [
        block_sum(diagonal[2 * k], diagonal[2 * k + 1], even_y, even_z) for k in range(-1, 3)
    ]
    inverse_coarse = [1.0 / d for d in coarse_diag]
    coarse_own = []
    for c in range(3):
        for k in range(2):
            total = block_sum(second[2 * k][c], second[2 * k + 1][c], tile_even_y, tile_even_z)
            coarse_own.append(coarse_damping * total * inverse_coarse[k + 1][0:8, 0:128])
    for t in range(6):
        own1[t] = coarse_own[t]
    z1[0] = pack(coarse_own)[0]
    group = flat_sends(own1, z1, ly1, lz1, lc1)

    arrive(group2)
    edges2 = []
    for n in range(2):
        edges2.append(jnp.concatenate([lz2[n], lc2[n]], 0))
        e2[6 + n] = edges2[n]
    mains2 = [jnp.concatenate([own_sa[t], ly2[t]], 0) for t in range(24)]
    for f in range(6):
        e2[f] = mains2[4 * f]

    arrive(group)
    edges1 = edges_beside(lz1, lc1, 0)
    mains1 = [jnp.concatenate([coarse_own[t], rows_beside(ly1, t)], 0) for t in range(6)]
    for t in range(6):
        e1[t] = mains1[t]
    e1[6] = edges1
    group = [
        send(e1, x1.at[0], device(-1, 0, 0)),
        send(e1, x1.at[1], device(1, 0, 0)),
    ]
    group2 = [send(e2, x2, device(-1, 0, 0))]
    arrive(group)
    coarse = {}
    for k in range(2):
        coarse[k - 2] = [widened(x1[1, 2 * c + k], x1[1, 6], 2 * c + k) * inside_low for c in range(3)]
        coarse[k] = [widened(mains1[2 * c + k], edges1, 2 * c + k) * inside for c in range(3)]
        coarse[k + 2] = [widened(x1[0, 2 * c + k], x1[0, 6], 2 * c + k) * inside_high for c in range(3)]
    spread = {p: coarse[p // 2] for p in range(-4, 8)}
    image = apply(spread, -2, 5)
    middle = {}
    for k in range(-1, 3):
        for c in range(3):
            total = block_sum(image[2 * k][c], image[2 * k + 1][c], even_y, even_z)
            fix = 2.0 * coarse[k][c] - coarse_damping * total * inverse_coarse[k + 1]
            for p in (2 * k, 2 * k + 1):
                middle.setdefault(p, []).append(first[p][c] + fix)
    image = apply(middle, -1, 4)
    direction = {
        p: [
            middle[p][c] + damping * (resid[p][c] - image[p][c]) * inverse_diag[p]
            for c in range(3)
        ]
        for p in range(-1, 5)
    }
    image = apply(direction, 0, 3)
    image = {p: [image[p][c][0:8, 0:128] for c in range(3)] for p in range(4)}
    numerator = denominator = None
    for p in range(4):
        for c in range(3):
            d = direction[p][c][0:8, 0:128]
            a, b = resid[p][c][0:8, 0:128] * d, d * image[p][c]
            numerator = a if numerator is None else numerator + a
            denominator = b if denominator is None else denominator + b
    numerator = numerator + pltpu.roll(numerator, 4, 0)
    denominator = denominator + pltpu.roll(denominator, 4, 0)
    sums = jnp.where(top_half, numerator, denominator)

    landed = [0]

    def spread_sums(stage, value, targets):
        ar_send[stage] = value
        base = landed[0]
        landed[0] += len(targets)
        group = [
            send(ar_send.at[stage], ar_land.at[base + n], target)
            for n, target in enumerate(targets)
        ]

        def gather():
            arrive(group)
            total = value
            for n in range(len(targets)):
                total = total + ar_land[base + n]
            return total

        return gather

    sums = spread_sums(0, sums, [partner()])()
    gather = spread_sums(1, sums, [device(2 * i, 0, 0) for i in (2, 1, -1)])
    arrive(group2)
    def ends(f, p):
        if p < 4:
            return widened(mains2[4 * f + p], edges2[(4 * f + p) // 16], 4 * f + p) * inside
        return widened(x2[f], x2[6 + (4 * f) // 16], 4 * f) * inside_high

    def corner_modes(fields):
        return [{m: v[0:8, 0:128] for m, v in forward(fields[p]).items()} for p in range(5)]

    adjoint_modes = corner_modes([[ends(c, p) for c in range(3)] for p in range(5)])
    state_modes = corner_modes([[ends(3 + c, p) for c in range(3)] for p in range(5)])
    direction_modes = corner_modes([direction[p] for p in range(5)])
    sens = []
    for p in range(4):
        force = stress(across(state_modes[p], state_modes[p + 1]))
        d = density[p][0:8, 0:128]
        weight = 3.0 * (1.0 - stiff_floor) * d * d * inverse_weight(p)[0:8, 0:128]
        for modes in (adjoint_modes, direction_modes):
            with_modes = across(modes[p], modes[p + 1])
            energy = None
            for mode, value in force.items():
                term = with_modes[mode] * value
                energy = term if energy is None else energy + term
            sens.append(weight * energy)
    for t in range(8):
        own3[t] = sens[t]
    z3[0] = pack(sens)[0]
    group = flat_sends(own3, z3, ly3, lz3, lc3)
    sums = gather()
    gather = spread_sums(2, sums, [device(2 * i, 0, 0) for i in (4, -4)])
    arrive(group)
    edges3 = edges_beside(lz3, lc3, 0)
    mains3 = [jnp.concatenate([sens[t], rows_beside(ly3, t)], 0) for t in range(8)]
    e3[0] = mains3[0]
    e3[1] = mains3[1]
    e3[2] = edges3
    e3[3] = mains3[6]
    e3[4] = mains3[7]
    group = [
        send(e3.at[pl.ds(0, 3)], x3.at[0], device(-1, 0, 0)),
        send(e3.at[pl.ds(2, 3)], x3.at[1], device(1, 0, 0)),
    ]
    sums = gather()
    gather = spread_sums(3, sums, [device(0, 0, k) for k in (4, 3, 5, 2, 6, 1, 7)])
    arrive(group)
    grads = []
    for f in range(2):
        planes = [widened(x3[1, 1 + f], x3[1, 0], 6 + f) * inside_low]
        planes += [widened(mains3[2 * p + f], edges3, 2 * p + f) * inside for p in range(4)]
        planes += [widened(x3[0, f], x3[0, 2], f) * inside_high]
        grads.append([v[0:8, 0:128] for v in smooth(planes)])
    sums = gather()
    sums = spread_sums(4, sums, [device(0, j, 0) for j in (2, 1, 3)])()
    numerator = jnp.sum(jnp.where(top_half, sums, 0.0), axis=(0, 1), keepdims=True)
    denominator = jnp.sum(jnp.where(top_half, 0.0, sums), axis=(0, 1), keepdims=True)
    step = jnp.broadcast_to(numerator / denominator, (8, 128))
    for p in range(4):
        for c in range(3):
            adjoint_out[c, p] = own_sa[4 * c + p] + step * direction[p][c][0:8, 0:128]
            resid_out[c, p] = own0[8 + 4 * c + p] - step * image[p][c]
        grad_out[p] = jnp.where(passive[p] == 0, grads[0][p] + step * grads[1][p], 0.0)
    for copy in copies:
        copy.wait_send()


def body(design, passive, fixed, state, adjoint, resid):
    def scratch(*shape):
        return pltpu.VMEM(shape, jnp.float32)

    n_copies = 8 + 8 + 3 + 8 + 2 + 1 + 16 + 8 + 2
    return pl.pallas_call(
        kernel,
        out_shape=(
            jax.ShapeDtypeStruct((3, 4, 8, 128), jnp.float32),
            jax.ShapeDtypeStruct((3, 4, 8, 128), jnp.float32),
            jax.ShapeDtypeStruct((4, 8, 128), jnp.float32),
        ),
        in_specs=[pl.BlockSpec(memory_space=pl.ANY)] * 6,
        out_specs=(pl.BlockSpec(memory_space=pltpu.VMEM),) * 3,
        scratch_shapes=[
            scratch(4, 8, 128),
            pltpu.VMEM((4, 8, 128), jnp.int32),
            pltpu.VMEM((4, 8, 128), jnp.int32),
            scratch(24, 8, 128),
            pltpu.SemaphoreType.DMA((6,)),
            scratch(20, 8, 128),
            scratch(2, 8, 128),
            scratch(20, 8, 128),
            scratch(2, 2, 8, 128),
            scratch(4, 2, 8, 128),
            scratch(8, 16, 128),
            scratch(3, 4, 16, 128),
            scratch(2, 16, 128),
            scratch(2, 4, 16, 128),
            scratch(2, 3, 16, 128),
            scratch(2, 3, 2, 16, 128),
            scratch(2, 2, 16, 128),
            scratch(2, 8, 128),
            scratch(24, 8, 128),
            scratch(2, 8, 128),
            scratch(2, 8, 128),
            scratch(8, 16, 128),
            scratch(8, 16, 128),
            scratch(6, 8, 128),
            scratch(1, 8, 128),
            scratch(6, 8, 128),
            scratch(2, 1, 8, 128),
            scratch(4, 1, 8, 128),
            scratch(7, 16, 128),
            scratch(2, 7, 16, 128),
            scratch(8, 8, 128),
            scratch(1, 8, 128),
            scratch(8, 8, 128),
            scratch(2, 1, 8, 128),
            scratch(4, 1, 8, 128),
            scratch(5, 16, 128),
            scratch(2, 3, 16, 128),
            scratch(5, 8, 128),
            scratch(16, 8, 128),
            pltpu.SemaphoreType.DMA((n_copies,)),
            pltpu.SemaphoreType.DMA((n_copies,)),
        ],
        compiler_params=pltpu.CompilerParams(
            collective_id=0, has_side_effects=True, vmem_limit_bytes=62 * 2**20
        ),
    )(
        design,
        passive,
        fixed,
        state.reshape(12, 8, 128),
        adjoint.reshape(12, 8, 128),
        resid.reshape(12, 8, 128),
    )


def solution(mesh):
    return jax.shard_map(
        body,
        mesh=mesh,
        in_specs=(P("gx", "gy", "gz"),) * 3 + (P(None, "gx", "gy", "gz"),) * 3,
        out_specs=(P(None, "gx", "gy", "gz"), P(None, "gx", "gy", "gz"), P("gx", "gy", "gz")),
        check_vma=False,
    )
```

```python
import math

import jax
import jax.numpy as jnp
from jax import lax
from jax.experimental import pallas as pl
from jax.experimental.pallas import tpu as pltpu
from jax.sharding import PartitionSpec as P

stiff_floor = 0.001
damping = 0.6
coarse_damping = 0.5

MESH = pl.DeviceIdType.MESH
AXES = ("gx", "gy", "gz")
GROUPS = (24, 4, 8)
EDGE = 1.0
FACE = 2.0 - math.sqrt(2.0)
CORNER = 2.0 - math.sqrt(3.0)

LAME = 0.3 / (1.3 * 0.4)
SHEAR = 0.5 / 1.3
NORMAL = (LAME + 2.0 * SHEAR) / 16.0
CROSS = LAME / 16.0
TWIST = SHEAR / 16.0
BEND = (LAME + 2.0 * SHEAR + SHEAR) / 48.0
BEND_CROSS = LAME / 48.0
SPIN = SHEAR / 48.0
HOUR = (LAME + 2.0 * SHEAR + 2.0 * SHEAR) / 144.0
NODE_DIAG = (LAME + 2.0 * SHEAR + 2.0 * SHEAR) / 9.0

BOX = [(i, j, k) for i in (-1, 0, 1) for j in (-1, 0, 1) for k in (-1, 0, 1)]
BOX = sorted((b for b in BOX if any(b)), key=lambda b: (-sum(map(abs, b)), b[0] == 0))


def device(dx, dy, dz):
    return tuple(
        lax.rem(lax.axis_index(axis) + (step + count), count)
        for axis, step, count in zip(AXES, (dx, dy, dz), GROUPS)
    )


def partner():
    place = lax.axis_index("gx")
    return (place + 1 - 2 * lax.rem(place, 2), lax.axis_index("gy"), lax.axis_index("gz"))


def zp(v):
    return pltpu.roll(v, v.shape[1] - 1, 1)


def zm(v):
    return pltpu.roll(v, 1, 1)


def yp(v):
    return pltpu.roll(v, v.shape[0] - 1, 0)


def ym(v):
    return pltpu.roll(v, 1, 0)


def forward(field):
    modes = {}
    for c in range(3):
        u = field[c]
        up = zp(u)
        for r, w in ((0, u + up), (1, up - u)):
            wp = yp(w)
            modes[c, 0, r] = w + wp
            modes[c, 1, r] = wp - w
    return modes


def across(low, high):
    modes = {}
    for (c, q, r), a in low.items():
        b = high[c, q, r]
        if (q, r) != (0, 0):
            modes[c, 0, q, r] = a + b
        modes[c, 1, q, r] = b - a
    return modes


def stress(u):
    f = {}
    total = (u[0, 1, 0, 0] + u[1, 0, 1, 0] + u[2, 0, 0, 1]) * CROSS
    for c, mode in ((0, (1, 0, 0)), (1, (0, 1, 0)), (2, (0, 0, 1))):
        f[(c,) + mode] = u[(c,) + mode] * (NORMAL - CROSS) + total
    for a, b in (
        ((0, 0, 0, 1), (2, 1, 0, 0)),
        ((0, 0, 1, 0), (1, 1, 0, 0)),
        ((1, 0, 0, 1), (2, 0, 1, 0)),
    ):
        f[a] = f[b] = (u[a] + u[b]) * TWIST
    total = u[0, 0, 1, 1] + u[1, 1, 0, 1] + u[2, 1, 1, 0]
    for a in ((0, 0, 1, 1), (1, 1, 0, 1), (2, 1, 1, 0)):
        f[a] = (u[a] + total) * SPIN
    for a, b in (
        ((0, 1, 0, 1), (1, 0, 1, 1)),
        ((0, 1, 1, 0), (2, 0, 1, 1)),
        ((1, 1, 1, 0), (2, 1, 0, 1)),
    ):
        f[a] = u[a] * BEND + u[b] * BEND_CROSS
        f[b] = u[b] * BEND + u[a] * BEND_CROSS
    for c in range(3):
        f[c, 1, 1, 1] = u[c, 1, 1, 1] * HOUR
    return f


def scaled(f, factor):
    out, seen = {}, {}
    for mode, value in f.items():
        if id(value) not in seen:
            seen[id(value)] = value * factor
        out[mode] = seen[id(value)]
    return out


def backward(modes):
    rows = []
    for c in range(3):
        lines = []
        for r in (0, 1):
            s, d = modes[c, 0, r], modes[c, 1, r]
            lines.append((s - d) + ym(s + d))
        rows.append((lines[0] - lines[1]) + zm(lines[0] + lines[1]))
    return rows


def operator(field, factor, free, span, known):
    result, carry, low = {}, None, None
    for p in span:
        held = [free[p] * u for u in field[p]]
        high = known[p] if p in known else forward(held)
        if low is not None:
            f = scaled(stress(across(low, high)), factor[p - 1])
            here, later = {}, {}
            for c, q, r in low:
                d = f[c, 1, q, r]
                if (q, r) == (0, 0):
                    here[c, q, r] = -d
                    later[c, q, r] = d
                else:
                    s = f[c, 0, q, r]
                    here[c, q, r] = s - d
                    later[c, q, r] = s + d
            if carry is not None:
                rows = backward({mode: carry[mode] + here[mode] for mode in here})
                result[p - 1] = [
                    free[p - 1] * rows[c] + (field[p - 1][c] - last[c]) for c in range(3)
                ]
            carry = later
        low, last = high, held
    return result


def smooth_plane(v):
    along_z = zp(v) + zm(v)
    along_y = yp(v) + ym(v)
    both = yp(along_z) + ym(along_z)
    sides = along_z + along_y
    return 2.0 * v + EDGE * sides + FACE * both, EDGE * v + FACE * sides + CORNER * both


def smooth(planes):
    parts = [smooth_plane(v) for v in planes]
    return [
        parts[p][0] + (parts[p - 1][1] + parts[p + 1][1]) for p in range(1, len(planes) - 1)
    ]


def block_sum(low, high, even_y, even_z):
    v = low + high
    v = v + jnp.where(even_z, zp(v), zm(v))
    return v + jnp.where(even_y, yp(v), ym(v))


def iota(shape, dim):
    return lax.broadcasted_iota(jnp.int32, shape, dim)


def pack(tiles):
    slot = iota((8, 128), 1) >> 3
    packs = []
    for first in range(0, len(tiles), 16):
        total = None
        for s, tile in enumerate(tiles[first : first + 16]):
            turned = pltpu.roll(tile, (4 + 8 * s) % 128, 1)
            total = turned if total is None else jnp.where(slot == s, turned, total)
        packs.append(total)
    return packs


def unpack(packed, s):
    return pltpu.roll(packed, (124 - 8 * (s % 16)) % 128, 1)


def kernel(
    design_hbm, passive_hbm, fixed_hbm, state_hbm, adjoint_hbm, resid_hbm,
    adjoint_out, resid_out, grad_out,
    design, passive, fixed, own_sa, in_sem,
    own0, z0, lx0, ly0, lz0, lc0,
    own1, z1, lx1, ly1, lz1, lc1,
    z2, lx2, ly2, lz2, lc2,
    own3, z3, lx3, ly3, lz3, lc3,
    ar_send, ar_land, send_sem, recv_sem, relay_sem,
):
    copies = []

    def send(src, dst, target):
        number = len(copies)
        copy = pltpu.make_async_remote_copy(
            src_ref=src,
            dst_ref=dst,
            send_sem=send_sem.at[number],
            recv_sem=recv_sem.at[number],
            device_id=target,
            device_id_type=MESH,
        )
        copy.start()
        copies.append(copy)
        return copy

    def arrive(group):
        for copy in group:
            copy.wait_recv()

    def greet(semaphore, friends):
        for friend in friends:
            pl.semaphore_signal(semaphore, inc=1, device_id=device(*friend), device_id_type=MESH)

    barrier = pltpu.get_barrier_semaphore()
    greet(barrier, BOX)

    pairs = [(design_hbm, design), (passive_hbm, passive), (fixed_hbm, fixed)]
    for p, first in ((0, 0), (1, 3), (2, 14), (3, 17)):
        pairs.append((resid_hbm.at[:, p], own0.at[pl.ds(first, 3)]))
    pairs += [(adjoint_hbm, own_sa.at[pl.ds(0, 3)]), (state_hbm, own_sa.at[pl.ds(3, 3)])]
    inputs = [pltpu.make_async_copy(src, dst, in_sem.at[n]) for n, (src, dst) in enumerate(pairs)]
    for copy in inputs:
        copy.start()

    place_x, place_y, place_z = (lax.axis_index(axis) for axis in AXES)
    wide = (16, 256)
    row, lane = iota(wide, 0), iota(wide, 1)
    at_y = place_y * 8 + jnp.where(row < 12, row, row - 16)
    at_z = place_z * 128 + jnp.where(lane < 192, lane, lane - 256)
    inside = ((at_y >= 0) & (at_y < 32) & (at_z >= 0) & (at_z < 1024)).astype(jnp.float32)
    inside_low = inside * (place_x > 0).astype(jnp.float32)
    inside_high = inside * (place_x < 23).astype(jnp.float32)

    def sides(dim_at, count):
        return (dim_at > 0).astype(jnp.float32) + (dim_at < count - 1).astype(jnp.float32)

    near_y, near_z = sides(at_y, 32), sides(at_z, 1024)
    near, nearer = near_y + near_z, near_y * near_z
    weight_base = 2.0 + EDGE * near + FACE * nearer
    weight_step = EDGE + FACE * near + CORNER * nearer
    inverse_inner = 1.0 / (weight_base + 2.0 * weight_step)
    inverse_end = 1.0 / (weight_base + weight_step)
    inverse_first = jnp.where(place_x > 0, inverse_inner, inverse_end)
    inverse_last = jnp.where(place_x < 23, inverse_inner, inverse_end)

    def inverse_weight(p):
        return inverse_first if p == 0 else inverse_last if p == 3 else inverse_inner

    even_y, even_z = (row & 1) == 0, (lane & 1) == 0
    tile_even_y, tile_even_z = (iota((8, 128), 0) & 1) == 0, (iota((8, 128), 1) & 1) == 0
    top_half = iota((8, 128), 0) < 4
    low_slot = (iota((8, 128), 1) & 7) < 4

    free_at, masked_at = (6, 7, 8, 13), (9, 10, 11, 12)

    def resid_at(c, p):
        return 3 * p + c + (8 if p > 1 else 0)

    for copy in inputs[:3]:
        copy.wait()
    for p in range(4):
        code = passive[p]
        own0[masked_at[p]] = jnp.where(code == 1, 0.0, jnp.where(code == 2, 1.0, design[p]))
        own0[free_at[p]] = (1 - fixed[p]).astype(jnp.float32)
    for copy in inputs[3:7]:
        copy.wait()
    for n, packed in enumerate(pack([own0[t] for t in range(20)])):
        z0[n] = packed
    pl.semaphore_wait(barrier, len(BOX))

    def exchange(own, edges, land, tiles, packs):
        land_x, land_y, land_z, land_c = land
        near, far = [], []
        for i, j, k in BOX:
            target, slot = device(i, j, k), i + 1
            if k == 0:
                span = pl.ds(*tiles[slot])
                if j == 0:
                    copy = send(own.at[span], land_x.at[slot // 2, span], target)
                else:
                    half = pl.ds(2 * (j + 1), 4)
                    copy = send(own.at[span, half], land_y.at[slot, span, half], target)
            else:
                span = pl.ds(*packs[slot])
                if j == 0:
                    copy = send(edges.at[span], land_z.at[slot, (k + 1) // 2, span], target)
                else:
                    corner = j + 1 + (k + 1) // 2
                    copy = send(edges.at[span], land_c.at[slot, corner, span], target)
            (near if i == 0 else far).append(copy)
        return near, far

    def main_of(own, land, slot, t):
        tile = own[t] if slot == 1 else land[0][slot // 2, t]
        return jnp.concatenate([tile, land[1][slot, t]], 0)

    def edges_of(land, slot, n):
        land_z, land_c = land[2], land[3]
        top = jnp.where(low_slot, land_z[slot, 1, n], land_z[slot, 0, n])
        from_low_y = jnp.where(low_slot, land_c[slot, 3, n], land_c[slot, 2, n])
        from_high_y = jnp.where(low_slot, land_c[slot, 1, n], land_c[slot, 0, n])
        return jnp.concatenate([top, jnp.where(top_half, from_high_y, from_low_y)], 0)

    def widened(main, packed, s):
        return jnp.concatenate([main, unpack(packed, s)], 1)

    masks = (inside_high, inside, inside_low)

    land0 = (lx0, ly0, lz0, lc0)
    near, far = exchange(own0, z0, land0, ((0, 12), (0, 20), (7, 13)), ((0, 1), (0, 2), (0, 2)))
    arrive(near)
    edges0 = {(1, n): edges_of(land0, 1, n) for n in range(2)}

    def input_plane(slot, t):
        return widened(main_of(own0, land0, slot, t), edges0[slot, t // 16], t) * masks[slot]

    masked = {p: input_plane(1, masked_at[p]) for p in range(4)}
    parts = {p: smooth_plane(masked[p]) for p in range(4)}
    free = {p: input_plane(1, free_at[p]) for p in range(4)}
    resid = {p: [input_plane(1, resid_at(c, p)) for c in range(3)] for p in range(4)}
    arrive(far)
    edges0[0, 0] = edges_of(land0, 0, 0)
    for n in range(2):
        edges0[2, n] = edges_of(land0, 2, n)
    for p in range(3):
        parts[p + 4] = smooth_plane(input_plane(0, masked_at[p]))
        free[p + 4] = input_plane(0, free_at[p])
    for p in range(4):
        parts[p - 4] = smooth_plane(input_plane(2, masked_at[p]))
    for p in range(1, 4):
        free[p - 4] = input_plane(2, free_at[p])
    for p in range(2):
        resid[p + 4] = [input_plane(0, resid_at(c, p)) for c in range(3)]
        resid[p - 2] = [input_plane(2, resid_at(c, p + 2)) for c in range(3)]
    greet(relay_sem.at[0], [(2, 0, 0), (-2, 0, 0)])
    greet(relay_sem.at[1], [(0, 0, 2), (0, 0, -2)])

    density, factor, paired = {}, {}, {}
    for p in range(-3, 6):
        d = (parts[p][0] + (parts[p - 1][1] + parts[p + 1][1])) * inverse_weight(p)
        density[p] = d
        f = stiff_floor + d * d * d * (1.0 - stiff_floor)
        factor[p] = f * (inside_low if p < 0 else inside if p < 4 else inside_high)
        v = factor[p] + zm(factor[p])
        paired[p] = v + ym(v)

    diagonal, inverse_diag, first = {}, {}, {}
    for p in range(-2, 6):
        diagonal[p] = free[p] * (NODE_DIAG * (paired[p] + paired[p - 1])) + (1.0 - free[p])
        inverse_diag[p] = 1.0 / diagonal[p]
        first[p] = [damping * resid[p][c] * inverse_diag[p] for c in range(3)]

    def apply(field, lowest, highest, known=None):
        span = range(lowest - 1, highest + 2)
        return operator(field, factor, free, span, known or {})

    image = apply(first, 0, 3)
    second = [
        [(resid[p][c] - image[p][c])[0:8, 0:128] for c in range(3)] for p in range(4)
    ]
    inverse_coarse = {}
    for k in range(2):
        total = block_sum(diagonal[2 * k], diagonal[2 * k + 1], even_y, even_z)
        inverse_coarse[k] = 1.0 / total
    coarse_own = []
    for k in range(2):
        for c in range(3):
            total = block_sum(second[2 * k][c], second[2 * k + 1][c], tile_even_y, tile_even_z)
            coarse_own.append(coarse_damping * total * inverse_coarse[k][0:8, 0:128])
    for t in range(6):
        own1[t] = coarse_own[t]
    z1[0] = pack(coarse_own)[0]
    land1 = (lx1, ly1, lz1, lc1)
    near, far = exchange(own1, z1, land1, ((0, 6),) * 3, ((0, 1),) * 3)

    for copy in inputs[7:]:
        copy.wait()
    for n, packed in enumerate(pack([own_sa[f, p] for p in range(4) for f in range(6)])):
        z2[n] = packed
    top_row = pl.ds(0, 1)
    group2 = [
        send(z2.at[pl.ds(0, 1)], lc2.at[1, pl.ds(0, 1)], device(-1, -1, -1)),
        send(z2, lc2.at[0], device(0, -1, -1)),
        send(z2.at[pl.ds(0, 1)], lz2.at[1, pl.ds(0, 1)], device(-1, 0, -1)),
        send(own_sa.at[:, 0, top_row], ly2.at[:, 4, top_row], device(-1, -1, 0)),
        send(own_sa.at[:, 0], lx2, device(-1, 0, 0)),
        send(own_sa.at[:, :, top_row], ly2.at[:, pl.ds(0, 4), top_row], device(0, -1, 0)),
        send(z2, lz2.at[0], device(0, 0, -1)),
    ]
    pl.semaphore_wait(relay_sem.at[0], 2)
    greet(relay_sem.at[2], [(4, 0, 0), (-4, 0, 0)])
    for k in (-1, 2):
        total = block_sum(diagonal[2 * k], diagonal[2 * k + 1], even_y, even_z)
        inverse_coarse[k] = 1.0 / total

    arrive(near)
    coarse = {}

    def coarse_plane(slot, k):
        edges = edges_of(land1, slot, 0)
        return [
            widened(main_of(own1, land1, slot, 3 * k + c), edges, 3 * k + c) * masks[slot]
            for c in range(3)
        ]

    for k in range(2):
        coarse[k] = coarse_plane(1, k)
    known = {p: forward([free[p] * u for u in coarse[p // 2]]) for p in range(4)}
    arrive(far)
    for k in range(2):
        coarse[k - 2] = coarse_plane(2, k)
        coarse[k + 2] = coarse_plane(0, k)
    pl.semaphore_wait(relay_sem.at[1], 2)
    pl.semaphore_wait(relay_sem.at[2], 2)
    greet(relay_sem.at[3], [(8, 0, 0), (-8, 0, 0)])
    spread = {p: coarse[p // 2] for p in range(-4, 8)}
    image = apply(spread, -2, 5, known)
    middle = {}
    for k in range(-1, 3):
        for c in range(3):
            total = block_sum(image[2 * k][c], image[2 * k + 1][c], even_y, even_z)
            fix = 2.0 * coarse[k][c] - coarse_damping * total * inverse_coarse[k]
            for p in (2 * k, 2 * k + 1):
                middle.setdefault(p, []).append(first[p][c] + fix)
    image = apply(middle, -1, 4)
    direction = {
        p: [
            middle[p][c] + damping * (resid[p][c] - image[p][c]) * inverse_diag[p]
            for c in range(3)
        ]
        for p in range(-1, 5)
    }
    image = apply(direction, 0, 3)
    image = {p: [image[p][c][0:8, 0:128] for c in range(3)] for p in range(4)}
    numerator = denominator = None
    for p in range(4):
        for c in range(3):
            d = direction[p][c][0:8, 0:128]
            a, b = resid[p][c][0:8, 0:128] * d, d * image[p][c]
            numerator = a if numerator is None else numerator + a
            denominator = b if denominator is None else denominator + b
    numerator = numerator + pltpu.roll(numerator, 4, 0)
    denominator = denominator + pltpu.roll(denominator, 4, 0)
    sums = jnp.where(top_half, numerator, denominator)

    landed = [0]

    def spread_sums(stage, value, targets):
        ar_send[stage] = value
        base = landed[0]
        landed[0] += len(targets)
        group = [
            send(ar_send.at[stage], ar_land.at[base + n], target)
            for n, target in enumerate(targets)
        ]

        def gather():
            arrive(group)
            total = value
            for n in range(len(targets)):
                total = total + ar_land[base + n]
            return total

        return gather

    sums = spread_sums(0, sums, [partner()])()
    pl.semaphore_wait(relay_sem.at[3], 2)
    gather = spread_sums(1, sums, [device(2 * i, 0, 0) for i in (6, 5, 7, 4, 8, 3, 9, 2, 10, 1, 11)])
    arrive(group2)

    edges2 = [jnp.concatenate([lz2[0, n], lc2[0, n]], 0) for n in range(2)]
    edges2_high = jnp.concatenate([lz2[1, 0], lc2[1, 0]], 0)

    def ends(f, p):
        if p < 4:
            main = jnp.concatenate([own_sa[f, p], ly2[f, p]], 0)
            return widened(main, edges2[(6 * p + f) // 16], 6 * p + f) * inside
        main = jnp.concatenate([lx2[f], ly2[f, 4]], 0)
        return widened(main, edges2_high, f) * inside_high

    def corner_modes(fields):
        return [{m: v[0:8, 0:128] for m, v in forward(fields[p]).items()} for p in range(5)]

    adjoint_modes = corner_modes([[ends(c, p) for c in range(3)] for p in range(5)])
    state_modes = corner_modes([[ends(3 + c, p) for c in range(3)] for p in range(5)])
    direction_modes = corner_modes([direction[p] for p in range(5)])
    sens = []
    for p in range(4):
        force = stress(across(state_modes[p], state_modes[p + 1]))
        d = density[p][0:8, 0:128]
        weight = 3.0 * (1.0 - stiff_floor) * d * d * inverse_weight(p)[0:8, 0:128]
        for modes in (adjoint_modes, direction_modes):
            with_modes = across(modes[p], modes[p + 1])
            energy = None
            for mode, value in force.items():
                term = with_modes[mode] * value
                energy = term if energy is None else energy + term
            sens.append(weight * energy)
    for t in range(8):
        own3[t] = sens[t]
    z3[0] = pack(sens)[0]
    land3 = (lx3, ly3, lz3, lc3)
    near, far = exchange(own3, z3, land3, ((0, 2), (0, 8), (6, 2)), ((0, 1),) * 3)
    sums = gather()
    gather = spread_sums(2, sums, [device(0, 0, k) for k in (4, 3, 5, 2, 6, 1, 7)])
    arrive(near)
    arrive(far)
    edges3 = [edges_of(land3, slot, 0) for slot in range(3)]

    def sens_plane(slot, t):
        return widened(main_of(own3, land3, slot, t), edges3[slot], t) * masks[slot]

    grads = []
    for f in range(2):
        planes = [sens_plane(2, 6 + f)]
        planes += [sens_plane(1, 2 * p + f) for p in range(4)]
        planes += [sens_plane(0, f)]
        grads.append([v[0:8, 0:128] for v in smooth(planes)])
    sums = gather()
    sums = spread_sums(3, sums, [device(0, j, 0) for j in (2, 1, 3)])()
    numerator = jnp.sum(jnp.where(top_half, sums, 0.0), axis=(0, 1), keepdims=True)
    denominator = jnp.sum(jnp.where(top_half, 0.0, sums), axis=(0, 1), keepdims=True)
    step = jnp.broadcast_to(numerator / denominator, (8, 128))
    for p in range(4):
        for c in range(3):
            adjoint_out[c, p] = own_sa[c, p] + step * direction[p][c][0:8, 0:128]
            resid_out[c, p] = own0[resid_at(c, p)] - step * image[p][c]
        grad_out[p] = jnp.where(passive[p] == 0, grads[0][p] + step * grads[1][p], 0.0)
    for copy in copies:
        copy.wait_send()


def body(design, passive, fixed, state, adjoint, resid):
    def scratch(*shape):
        return pltpu.VMEM(shape, jnp.float32)

    def landing(tiles, packs):
        return [
            scratch(2, tiles, 8, 128),
            scratch(3, tiles, 8, 128),
            scratch(3, 2, packs, 8, 128),
            scratch(3, 4, packs, 8, 128),
        ]

    n_copies = 3 * 26 + 7 + 22
    return pl.pallas_call(
        kernel,
        out_shape=(
            pltpu.VMEM((3, 4, 8, 128), jnp.float32),
            pltpu.VMEM((3, 4, 8, 128), jnp.float32),
            pltpu.VMEM((4, 8, 128), jnp.float32),
        ),
        in_specs=[pl.BlockSpec(memory_space=pl.ANY)] * 6,
        out_specs=(pl.BlockSpec(memory_space=pltpu.VMEM),) * 3,
        scratch_shapes=[
            scratch(4, 8, 128),
            pltpu.VMEM((4, 8, 128), jnp.int32),
            pltpu.VMEM((4, 8, 128), jnp.int32),
            scratch(6, 4, 8, 128),
            pltpu.SemaphoreType.DMA((9,)),
            scratch(20, 8, 128),
            scratch(2, 8, 128),
            *landing(20, 2),
            scratch(6, 8, 128),
            scratch(1, 8, 128),
            *landing(6, 1),
            scratch(2, 8, 128),
            scratch(6, 8, 128),
            scratch(6, 5, 8, 128),
            scratch(2, 2, 8, 128),
            scratch(2, 2, 8, 128),
            scratch(8, 8, 128),
            scratch(1, 8, 128),
            *landing(8, 1),
            scratch(4, 8, 128),
            scratch(22, 8, 128),
            pltpu.SemaphoreType.DMA((n_copies,)),
            pltpu.SemaphoreType.DMA((n_copies,)),
            pltpu.SemaphoreType.REGULAR((4,)),
        ],
        compiler_params=pltpu.CompilerParams(
            collective_id=0, has_side_effects=True, vmem_limit_bytes=62 * 2**20
        ),
    )(design, passive, fixed, state, adjoint, resid)


def solution(mesh):
    return jax.shard_map(
        body,
        mesh=mesh,
        in_specs=(P("gx", "gy", "gz"),) * 3 + (P(None, "gx", "gy", "gz"),) * 3,
        out_specs=(P(None, "gx", "gy", "gz"), P(None, "gx", "gy", "gz"), P("gx", "gy", "gz")),
        check_vma=False,
    )
```

```python
import math

import jax
import jax.numpy as jnp
from jax import lax
from jax.experimental import pallas as pl
from jax.experimental.pallas import tpu as pltpu
from jax.sharding import PartitionSpec as P

stiff_floor = 0.001
damping = 0.6
coarse_damping = 0.5

MESH = pl.DeviceIdType.MESH
AXES = ("gx", "gy", "gz")
GROUPS = (24, 4, 8)
EDGE = 1.0
FACE = 2.0 - math.sqrt(2.0)
CORNER = 2.0 - math.sqrt(3.0)

LAME = 0.3 / (1.3 * 0.4)
SHEAR = 0.5 / 1.3
NORMAL = (LAME + 2.0 * SHEAR) / 16.0
CROSS = LAME / 16.0
TWIST = SHEAR / 16.0
BEND = (LAME + 2.0 * SHEAR + SHEAR) / 48.0
BEND_CROSS = LAME / 48.0
SPIN = SHEAR / 48.0
HOUR = (LAME + 2.0 * SHEAR + 2.0 * SHEAR) / 144.0
NODE_DIAG = (LAME + 2.0 * SHEAR + 2.0 * SHEAR) / 9.0

BOX = [(i, j, k) for i in (-1, 0, 1) for j in (-1, 0, 1) for k in (-1, 0, 1)]
BOX = sorted((b for b in BOX if any(b)), key=lambda b: (-sum(map(abs, b)), b[0] == 0))


def device(dx, dy, dz):
    return tuple(
        lax.rem(lax.axis_index(axis) + (step + count), count)
        for axis, step, count in zip(AXES, (dx, dy, dz), GROUPS)
    )


def partner():
    place = lax.axis_index("gx")
    return (place + 1 - 2 * lax.rem(place, 2), lax.axis_index("gy"), lax.axis_index("gz"))


def zp(v):
    return pltpu.roll(v, v.shape[1] - 1, 1)


def zm(v):
    return pltpu.roll(v, 1, 1)


def yp(v):
    return pltpu.roll(v, v.shape[0] - 1, 0)


def ym(v):
    return pltpu.roll(v, 1, 0)


def forward(field):
    modes = {}
    for c in range(3):
        u = field[c]
        up = zp(u)
        for r, w in ((0, u + up), (1, up - u)):
            wp = yp(w)
            modes[c, 0, r] = w + wp
            modes[c, 1, r] = wp - w
    return modes


def across(low, high):
    modes = {}
    for (c, q, r), a in low.items():
        b = high[c, q, r]
        if (q, r) != (0, 0):
            modes[c, 0, q, r] = a + b
        modes[c, 1, q, r] = b - a
    return modes


def stress(u):
    f = {}
    total = (u[0, 1, 0, 0] + u[1, 0, 1, 0] + u[2, 0, 0, 1]) * CROSS
    for c, mode in ((0, (1, 0, 0)), (1, (0, 1, 0)), (2, (0, 0, 1))):
        f[(c,) + mode] = u[(c,) + mode] * (NORMAL - CROSS) + total
    for a, b in (
        ((0, 0, 0, 1), (2, 1, 0, 0)),
        ((0, 0, 1, 0), (1, 1, 0, 0)),
        ((1, 0, 0, 1), (2, 0, 1, 0)),
    ):
        f[a] = f[b] = (u[a] + u[b]) * TWIST
    total = u[0, 0, 1, 1] + u[1, 1, 0, 1] + u[2, 1, 1, 0]
    for a in ((0, 0, 1, 1), (1, 1, 0, 1), (2, 1, 1, 0)):
        f[a] = (u[a] + total) * SPIN
    for a, b in (
        ((0, 1, 0, 1), (1, 0, 1, 1)),
        ((0, 1, 1, 0), (2, 0, 1, 1)),
        ((1, 1, 1, 0), (2, 1, 0, 1)),
    ):
        f[a] = u[a] * BEND + u[b] * BEND_CROSS
        f[b] = u[b] * BEND + u[a] * BEND_CROSS
    for c in range(3):
        f[c, 1, 1, 1] = u[c, 1, 1, 1] * HOUR
    return f


def scaled(f, factor):
    out, seen = {}, {}
    for mode, value in f.items():
        if id(value) not in seen:
            seen[id(value)] = value * factor
        out[mode] = seen[id(value)]
    return out


def backward(modes):
    rows = []
    for c in range(3):
        lines = []
        for r in (0, 1):
            s, d = modes[c, 0, r], modes[c, 1, r]
            lines.append((s - d) + ym(s + d))
        rows.append((lines[0] - lines[1]) + zm(lines[0] + lines[1]))
    return rows


def operator(field, factor, free, span, known, ready):
    result, carry, low = {}, None, None
    for p in span:
        held = [free[p] * u for u in field[p]]
        high = known[p] if p in known else forward(held)
        if low is not None:
            if p - 1 in ready:
                f = ready[p - 1]
            else:
                f = scaled(stress(across(low, high)), factor[p - 1])
            here, later = {}, {}
            for c, q, r in low:
                d = f[c, 1, q, r]
                if (q, r) == (0, 0):
                    here[c, q, r] = -d
                    later[c, q, r] = d
                else:
                    s = f[c, 0, q, r]
                    here[c, q, r] = s - d
                    later[c, q, r] = s + d
            if carry is not None:
                rows = backward({mode: carry[mode] + here[mode] for mode in here})
                result[p - 1] = [
                    free[p - 1] * rows[c] + (field[p - 1][c] - last[c]) for c in range(3)
                ]
            carry = later
        low, last = high, held
    return result


def smooth_plane(v):
    along_z = zp(v) + zm(v)
    along_y = yp(v) + ym(v)
    both = yp(along_z) + ym(along_z)
    sides = along_z + along_y
    return 2.0 * v + EDGE * sides + FACE * both, EDGE * v + FACE * sides + CORNER * both


def smooth(planes):
    parts = [smooth_plane(v) for v in planes]
    return [
        parts[p][0] + (parts[p - 1][1] + parts[p + 1][1]) for p in range(1, len(planes) - 1)
    ]


def block_sum(low, high, even_y, even_z):
    v = low + high
    v = v + jnp.where(even_z, zp(v), zm(v))
    return v + jnp.where(even_y, yp(v), ym(v))


def iota(shape, dim):
    return lax.broadcasted_iota(jnp.int32, shape, dim)


def pack(tiles):
    slot = iota((8, 128), 1) >> 3
    packs = []
    for first in range(0, len(tiles), 16):
        total = None
        for s, tile in enumerate(tiles[first : first + 16]):
            turned = pltpu.roll(tile, (4 + 8 * s) % 128, 1)
            total = turned if total is None else jnp.where(slot == s, turned, total)
        packs.append(total)
    return packs


def unpack(packed, s):
    return pltpu.roll(packed, (124 - 8 * (s % 16)) % 128, 1)


def kernel(
    design_hbm, passive_hbm, fixed_hbm, state_hbm, adjoint_hbm, resid_hbm,
    direction_out, image_out, grads_out, step_out,
    design, passive, fixed, own_sa, in_sem,
    own0, z0, lx0, ly0, lz0, lc0,
    own1, z1, lx1, ly1, lz1, lc1,
    z2, lx2, ly2, lz2, lc2,
    own3, z3, lx3, ly3, lz3, lc3,
    ar_send, ar_land, send_sem, recv_sem, relay_sem,
):
    copies, sent = [], [0]

    def settle():
        for copy in copies[sent[0] :]:
            copy.wait_send()
        sent[0] = len(copies)

    def send(src, dst, target):
        number = len(copies)
        copy = pltpu.make_async_remote_copy(
            src_ref=src,
            dst_ref=dst,
            send_sem=send_sem.at[number],
            recv_sem=recv_sem.at[number],
            device_id=target,
            device_id_type=MESH,
        )
        copy.start()
        copies.append(copy)
        return copy

    def arrive(group):
        for copy in group:
            copy.wait_recv()

    def greet(semaphore, friends):
        for friend in friends:
            pl.semaphore_signal(semaphore, inc=1, device_id=device(*friend), device_id_type=MESH)

    pairs = [(design_hbm, design), (passive_hbm, passive), (fixed_hbm, fixed)]
    for p, first in ((0, 0), (1, 3), (2, 14), (3, 17)):
        pairs.append((resid_hbm.at[:, p], own0.at[pl.ds(first, 3)]))
    pairs += [(adjoint_hbm, own_sa.at[pl.ds(0, 3)]), (state_hbm, own_sa.at[pl.ds(3, 3)])]
    inputs = [pltpu.make_async_copy(src, dst, in_sem.at[n]) for n, (src, dst) in enumerate(pairs)]
    for copy in inputs:
        copy.start()

    barrier = pltpu.get_barrier_semaphore()
    greeted = BOX + [(2, 0, 0), (-2, 0, 0)]
    greet(barrier, greeted)

    place_x, place_y, place_z = (lax.axis_index(axis) for axis in AXES)
    wide = (16, 256)
    row, lane = iota(wide, 0), iota(wide, 1)
    at_y = place_y * 8 + jnp.where(row < 12, row, row - 16)
    at_z = place_z * 128 + jnp.where(lane < 192, lane, lane - 256)
    inside = ((at_y >= 0) & (at_y < 32) & (at_z >= 0) & (at_z < 1024)).astype(jnp.float32)
    inside_low = inside * (place_x > 0).astype(jnp.float32)
    inside_high = inside * (place_x < 23).astype(jnp.float32)

    def sides(dim_at, count):
        return (dim_at > 0).astype(jnp.float32) + (dim_at < count - 1).astype(jnp.float32)

    near_y, near_z = sides(at_y, 32), sides(at_z, 1024)
    near, nearer = near_y + near_z, near_y * near_z
    weight_base = 2.0 + EDGE * near + FACE * nearer
    weight_step = EDGE + FACE * near + CORNER * nearer
    inverse_inner = 1.0 / (weight_base + 2.0 * weight_step)
    inverse_end = 1.0 / (weight_base + weight_step)
    inverse_first = jnp.where(place_x > 0, inverse_inner, inverse_end)
    inverse_last = jnp.where(place_x < 23, inverse_inner, inverse_end)

    def inverse_weight(p):
        return inverse_first if p == 0 else inverse_last if p == 3 else inverse_inner

    even_y, even_z = (row & 1) == 0, (lane & 1) == 0
    tile_even_y, tile_even_z = (iota((8, 128), 0) & 1) == 0, (iota((8, 128), 1) & 1) == 0
    top_half = iota((8, 128), 0) < 4
    low_slot = (iota((8, 128), 1) & 7) < 4

    free_at, masked_at = (6, 7, 8, 13), (9, 10, 11, 12)

    def resid_at(c, p):
        return 3 * p + c + (8 if p > 1 else 0)

    for copy in inputs[:3]:
        copy.wait()
    for p in range(4):
        code = passive[p]
        own0[masked_at[p]] = jnp.where(code == 1, 0.0, jnp.where(code == 2, 1.0, design[p]))
        own0[free_at[p]] = (1 - fixed[p]).astype(jnp.float32)
    for copy in inputs[3:7]:
        copy.wait()
    for n, packed in enumerate(pack([own0[t] for t in range(20)])):
        z0[n] = packed
    pl.semaphore_wait(barrier, len(greeted))

    def exchange(own, edges, land, tiles, packs):
        land_x, land_y, land_z, land_c = land
        near, far = [], []
        for i, j, k in BOX:
            target, slot = device(i, j, k), i + 1
            if k == 0:
                span = pl.ds(*tiles[slot])
                if j == 0:
                    copy = send(own.at[span], land_x.at[slot // 2, span], target)
                else:
                    half = pl.ds(2 * (j + 1), 4)
                    copy = send(own.at[span, half], land_y.at[slot, span, half], target)
            else:
                span = pl.ds(*packs[slot])
                if j == 0:
                    copy = send(edges.at[span], land_z.at[slot, (k + 1) // 2, span], target)
                else:
                    corner = j + 1 + (k + 1) // 2
                    copy = send(edges.at[span], land_c.at[slot, corner, span], target)
            (near if i == 0 else far).append(copy)
        return near, far

    def main_of(own, land, slot, t):
        tile = own[t] if slot == 1 else land[0][slot // 2, t]
        return jnp.concatenate([tile, land[1][slot, t]], 0)

    def edges_of(land, slot, n):
        land_z, land_c = land[2], land[3]
        top = jnp.where(low_slot, land_z[slot, 1, n], land_z[slot, 0, n])
        from_low_y = jnp.where(low_slot, land_c[slot, 3, n], land_c[slot, 2, n])
        from_high_y = jnp.where(low_slot, land_c[slot, 1, n], land_c[slot, 0, n])
        return jnp.concatenate([top, jnp.where(top_half, from_high_y, from_low_y)], 0)

    def widened(main, packed, s):
        return jnp.concatenate([main, unpack(packed, s)], 1)

    masks = (inside_high, inside, inside_low)

    land0 = (lx0, ly0, lz0, lc0)
    near, far = exchange(own0, z0, land0, ((0, 12), (0, 20), (7, 13)), ((0, 1), (0, 2), (0, 2)))
    greet(relay_sem.at[0], [(2, 0, 0), (-2, 0, 0)])
    arrive(near)
    edges0 = {(1, n): edges_of(land0, 1, n) for n in range(2)}

    def input_plane(slot, t):
        return widened(main_of(own0, land0, slot, t), edges0[slot, t // 16], t) * masks[slot]

    masked = {p: input_plane(1, masked_at[p]) for p in range(4)}
    parts = {p: smooth_plane(masked[p]) for p in range(4)}
    free = {p: input_plane(1, free_at[p]) for p in range(4)}
    resid = {p: [input_plane(1, resid_at(c, p)) for c in range(3)] for p in range(4)}
    density, factor, paired = {}, {}, {}
    diagonal, inverse_diag, first = {}, {}, {}
    arrive(far)
    edges0[0, 0] = edges_of(land0, 0, 0)
    for n in range(2):
        edges0[2, n] = edges_of(land0, 2, n)
    greet(relay_sem.at[1], [(0, 0, 2), (0, 0, -2)])
    pl.semaphore_wait(relay_sem.at[0], 2)
    greet(relay_sem.at[2], [(4, 0, 0), (-4, 0, 0)])

    def beyond(p):
        return (2, p + 4) if p < 0 else (0, p - 4)

    def take_masked(p):
        slot, q = beyond(p)
        parts[p] = smooth_plane(input_plane(slot, masked_at[q]))

    def take_nodes(p):
        slot, q = beyond(p)
        free[p] = input_plane(slot, free_at[q])
        if -3 < p < 6:
            resid[p] = [input_plane(slot, resid_at(c, q)) for c in range(3)]

    def take_element(p):
        d = (parts[p][0] + (parts[p - 1][1] + parts[p + 1][1])) * inverse_weight(p)
        density[p] = d
        f = stiff_floor + d * d * d * (1.0 - stiff_floor)
        factor[p] = f * (inside_low if p < 0 else inside if p < 4 else inside_high)
        v = factor[p] + zm(factor[p])
        paired[p] = v + ym(v)

    def take_diagonal(p):
        diagonal[p] = free[p] * (NODE_DIAG * (paired[p] + paired[p - 1])) + (1.0 - free[p])
        inverse_diag[p] = 1.0 / diagonal[p]
        first[p] = [damping * resid[p][c] * inverse_diag[p] for c in range(3)]

    for p in (-3, -2, -1, 4, 5):
        take_masked(p)
    for p in (-1, 4):
        take_nodes(p)
    for p in range(-2, 5):
        if p not in density:
            take_element(p)
    for p in range(-1, 5):
        take_diagonal(p)

    def apply(field, lowest, highest, known=None, ready=None):
        span = range(lowest - 1, highest + 2)
        return operator(field, factor, free, span, known or {}, ready or {})

    image = apply(first, 0, 3)
    second = [
        [(resid[p][c] - image[p][c])[0:8, 0:128] for c in range(3)] for p in range(4)
    ]
    inverse_coarse = {}
    for k in range(2):
        total = block_sum(diagonal[2 * k], diagonal[2 * k + 1], even_y, even_z)
        inverse_coarse[k] = 1.0 / total
    coarse_own = []
    for k in range(2):
        for c in range(3):
            total = block_sum(second[2 * k][c], second[2 * k + 1][c], tile_even_y, tile_even_z)
            coarse_own.append(coarse_damping * total * inverse_coarse[k][0:8, 0:128])
    for t in range(6):
        own1[t] = coarse_own[t]
    z1[0] = pack(coarse_own)[0]
    land1 = (lx1, ly1, lz1, lc1)
    near, far = exchange(own1, z1, land1, ((0, 6),) * 3, ((0, 1),) * 3)

    for copy in inputs[7:]:
        copy.wait()
    for n, packed in enumerate(pack([own_sa[f, p] for p in range(4) for f in range(6)])):
        z2[n] = packed
    top_row = pl.ds(0, 1)
    group2 = [
        send(z2.at[pl.ds(0, 1)], lc2.at[1, pl.ds(0, 1)], device(-1, -1, -1)),
        send(z2, lc2.at[0], device(0, -1, -1)),
        send(z2.at[pl.ds(0, 1)], lz2.at[1, pl.ds(0, 1)], device(-1, 0, -1)),
        send(own_sa.at[:, 0, top_row], ly2.at[:, 4, top_row], device(-1, -1, 0)),
        send(own_sa.at[:, 0], lx2, device(-1, 0, 0)),
        send(own_sa.at[:, :, top_row], ly2.at[:, pl.ds(0, 4), top_row], device(0, -1, 0)),
        send(z2, lz2.at[0], device(0, 0, -1)),
    ]
    pl.semaphore_wait(relay_sem.at[2], 2)
    greet(relay_sem.at[3], [(8, 0, 0), (-8, 0, 0)])
    for p in (-4, 6):
        take_masked(p)
    for p in (-3, -2, 5, 6):
        take_nodes(p)
    for p in (-3, 5):
        take_element(p)
    for p in (-2, 5):
        take_diagonal(p)
    for k in (-1, 2):
        total = block_sum(diagonal[2 * k], diagonal[2 * k + 1], even_y, even_z)
        inverse_coarse[k] = 1.0 / total

    arrive(near)
    coarse = {}

    def coarse_plane(slot, k):
        edges = edges_of(land1, slot, 0)
        return [
            widened(main_of(own1, land1, slot, 3 * k + c), edges, 3 * k + c) * masks[slot]
            for c in range(3)
        ]

    for k in range(2):
        coarse[k] = coarse_plane(1, k)
    known = {p: forward([free[p] * u for u in coarse[p // 2]]) for p in range(4)}
    ready = {p: scaled(stress(across(known[p], known[p + 1])), factor[p]) for p in range(3)}
    arrive(far)
    for k in range(2):
        coarse[k - 2] = coarse_plane(2, k)
        coarse[k + 2] = coarse_plane(0, k)
    pl.semaphore_wait(relay_sem.at[1], 2)
    spread = {p: coarse[p // 2] for p in range(-4, 8)}
    image = apply(spread, -2, 5, known, ready)
    middle = {}
    for k in range(-1, 3):
        for c in range(3):
            total = block_sum(image[2 * k][c], image[2 * k + 1][c], even_y, even_z)
            fix = 2.0 * coarse[k][c] - coarse_damping * total * inverse_coarse[k]
            for p in (2 * k, 2 * k + 1):
                middle.setdefault(p, []).append(first[p][c] + fix)
    direction = {}

    def smoothed_again(lowest, highest):
        image = apply(middle, lowest, highest)
        for p in range(lowest, highest + 1):
            direction[p] = [
                middle[p][c] + damping * (resid[p][c] - image[p][c]) * inverse_diag[p]
                for c in range(3)
            ]

    smoothed_again(0, 4)
    held_modes = {p: forward([free[p] * d for d in direction[p]]) for p in range(5)}
    numerator = denominator = None
    for p in range(4):
        u = across(*({m: v[0:8, 0:128] for m, v in held_modes[p + n].items()} for n in range(2)))
        energy = None
        for mode, value in stress(u).items():
            term = u[mode] * value
            energy = term if energy is None else energy + term
        b = factor[p][0:8, 0:128] * energy
        fixed_part = None
        for c in range(3):
            d = direction[p][c][0:8, 0:128]
            direction_out[c, p] = d
            a = resid[p][c][0:8, 0:128] * d
            numerator = a if numerator is None else numerator + a
            fixed_part = d * d if fixed_part is None else fixed_part + d * d
        b = b + (1.0 - free[p][0:8, 0:128]) * fixed_part
        denominator = b if denominator is None else denominator + b
    numerator = numerator + pltpu.roll(numerator, 4, 0)
    denominator = denominator + pltpu.roll(denominator, 4, 0)
    sums = jnp.where(top_half, numerator, denominator)

    landed = [0]

    def spread_sums(stage, value, targets):
        ar_send[stage] = value
        base = landed[0]
        landed[0] += len(targets)
        group = [
            send(ar_send.at[stage], ar_land.at[base + n], target)
            for n, target in enumerate(targets)
        ]

        def gather():
            arrive(group)
            total = value
            for n in range(len(targets)):
                total = total + ar_land[base + n]
            return total

        return gather

    sums = spread_sums(0, sums, [partner()])()
    gather = spread_sums(1, sums, [device(0, 0, k) for k in (4, 3, 5, 2, 6, 1, 7)])
    arrive(group2)

    edges2 = [jnp.concatenate([lz2[0, n], lc2[0, n]], 0) for n in range(2)]
    edges2_high = jnp.concatenate([lz2[1, 0], lc2[1, 0]], 0)

    def ends(f, p):
        if p < 4:
            main = jnp.concatenate([own_sa[f, p], ly2[f, p]], 0)
            return widened(main, edges2[(6 * p + f) // 16], 6 * p + f) * inside
        main = jnp.concatenate([lx2[f], ly2[f, 4]], 0)
        return widened(main, edges2_high, f) * inside_high

    def corner_modes(fields):
        return [{m: v[0:8, 0:128] for m, v in forward(fields[p]).items()} for p in range(5)]

    adjoint_modes = corner_modes([[ends(c, p) for c in range(3)] for p in range(5)])
    state_modes = corner_modes([[ends(3 + c, p) for c in range(3)] for p in range(5)])
    direction_modes = corner_modes([direction[p] for p in range(5)])
    sens = []
    for p in range(4):
        force = stress(across(state_modes[p], state_modes[p + 1]))
        d = density[p][0:8, 0:128]
        weight = 3.0 * (1.0 - stiff_floor) * d * d * inverse_weight(p)[0:8, 0:128]
        for modes in (adjoint_modes, direction_modes):
            with_modes = across(modes[p], modes[p + 1])
            energy = None
            for mode, value in force.items():
                term = with_modes[mode] * value
                energy = term if energy is None else energy + term
            sens.append(weight * energy)
    for t in range(8):
        own3[t] = sens[t]
    z3[0] = pack(sens)[0]
    land3 = (lx3, ly3, lz3, lc3)
    settle()
    near, far = exchange(own3, z3, land3, ((0, 2), (0, 8), (6, 2)), ((0, 1),) * 3)
    smoothed_again(-1, -1)
    image = apply(direction, 0, 3, held_modes)
    for p in range(4):
        for c in range(3):
            image_out[c, p] = image[p][c][0:8, 0:128]
    sums = gather()
    sums = spread_sums(2, sums, [device(0, j, 0) for j in (2, 1, 3)])()
    pl.semaphore_wait(relay_sem.at[3], 2)
    gather = spread_sums(3, sums, [device(2 * i, 0, 0) for i in (6, 5, 7, 4, 8, 3, 9, 2, 10, 1, 11)])
    arrive(near)
    arrive(far)
    edges3 = [edges_of(land3, slot, 0) for slot in range(3)]

    def sens_plane(slot, t):
        return widened(main_of(own3, land3, slot, t), edges3[slot], t) * masks[slot]

    for f in range(2):
        planes = [sens_plane(2, 6 + f)]
        planes += [sens_plane(1, 2 * p + f) for p in range(4)]
        planes += [sens_plane(0, f)]
        for p, v in enumerate(smooth(planes)):
            grads_out[f, p] = v[0:8, 0:128]
    settle()
    sums = gather()
    numerator = jnp.sum(jnp.where(top_half, sums, 0.0), axis=(0, 1), keepdims=True)
    denominator = jnp.sum(jnp.where(top_half, 0.0, sums), axis=(0, 1), keepdims=True)
    step_out[...] = jnp.broadcast_to(numerator / denominator, (8, 128))
    settle()


def body(design, passive, fixed, state, adjoint, resid):
    def scratch(*shape):
        return pltpu.VMEM(shape, jnp.float32)

    def landing(tiles, packs):
        return [
            scratch(2, tiles, 8, 128),
            scratch(3, tiles, 8, 128),
            scratch(3, 2, packs, 8, 128),
            scratch(3, 4, packs, 8, 128),
        ]

    n_copies = 3 * 26 + 7 + 22
    direction, image, grads, step = pl.pallas_call(
        kernel,
        out_shape=(
            pltpu.VMEM((3, 4, 8, 128), jnp.float32),
            pltpu.VMEM((3, 4, 8, 128), jnp.float32),
            pltpu.VMEM((2, 4, 8, 128), jnp.float32),
            pltpu.VMEM((8, 128), jnp.float32),
        ),
        in_specs=[pl.BlockSpec(memory_space=pl.ANY)] * 6,
        out_specs=(pl.BlockSpec(memory_space=pltpu.VMEM),) * 4,
        scratch_shapes=[
            scratch(4, 8, 128),
            pltpu.VMEM((4, 8, 128), jnp.int32),
            pltpu.VMEM((4, 8, 128), jnp.int32),
            scratch(6, 4, 8, 128),
            pltpu.SemaphoreType.DMA((9,)),
            scratch(20, 8, 128),
            scratch(2, 8, 128),
            *landing(20, 2),
            scratch(6, 8, 128),
            scratch(1, 8, 128),
            *landing(6, 1),
            scratch(2, 8, 128),
            scratch(6, 8, 128),
            scratch(6, 5, 8, 128),
            scratch(2, 2, 8, 128),
            scratch(2, 2, 8, 128),
            scratch(8, 8, 128),
            scratch(1, 8, 128),
            *landing(8, 1),
            scratch(4, 8, 128),
            scratch(22, 8, 128),
            pltpu.SemaphoreType.DMA((n_copies,)),
            pltpu.SemaphoreType.DMA((n_copies,)),
            pltpu.SemaphoreType.REGULAR((4,)),
        ],
        compiler_params=pltpu.CompilerParams(
            collective_id=0, has_side_effects=True, vmem_limit_bytes=62 * 2**20
        ),
    )(design, passive, fixed, state, adjoint, resid)
    return (
        adjoint + step * direction,
        resid - step * image,
        jnp.where(passive == 0, grads[0] + step * grads[1], 0.0),
    )


def solution(mesh):
    return jax.shard_map(
        body,
        mesh=mesh,
        in_specs=(P("gx", "gy", "gz"),) * 3 + (P(None, "gx", "gy", "gz"),) * 3,
        out_specs=(P(None, "gx", "gy", "gz"), P(None, "gx", "gy", "gz"), P("gx", "gy", "gz")),
        check_vma=False,
    )
```

```python
import math

import jax
import jax.numpy as jnp
from jax import lax
from jax.experimental import pallas as pl
from jax.experimental.pallas import tpu as pltpu
from jax.sharding import PartitionSpec as P

stiff_floor = 0.001
damping = 0.6
coarse_damping = 0.5

MESH = pl.DeviceIdType.MESH
AXES = ("gx", "gy", "gz")
GROUPS = (24, 4, 8)
EDGE = 1.0
FACE = 2.0 - math.sqrt(2.0)
CORNER = 2.0 - math.sqrt(3.0)

LAME = 0.3 / (1.3 * 0.4)
SHEAR = 0.5 / 1.3
NORMAL = (LAME + 2.0 * SHEAR) / 16.0
CROSS = LAME / 16.0
TWIST = SHEAR / 16.0
BEND = (LAME + 2.0 * SHEAR + SHEAR) / 48.0
BEND_CROSS = LAME / 48.0
SPIN = SHEAR / 48.0
HOUR = (LAME + 2.0 * SHEAR + 2.0 * SHEAR) / 144.0
NODE_DIAG = (LAME + 2.0 * SHEAR + 2.0 * SHEAR) / 9.0

BOX = [(i, j, k) for i in (-1, 0, 1) for j in (-1, 0, 1) for k in (-1, 0, 1)]
BOX = sorted((b for b in BOX if any(b)), key=lambda b: (-sum(map(abs, b)), b[0] == 0))

FLAT = [(j, k) for j in range(4) for k in range(8) if j or k]
FLAT.sort(key=lambda t: -min(t[0], 4 - t[0]) - min(t[1], 8 - t[1]))
LINE = sorted(range(1, 24), key=lambda i: -min(i, 24 - i))


def device(dx, dy, dz):
    return tuple(
        lax.rem(lax.axis_index(axis) + (step + count), count)
        for axis, step, count in zip(AXES, (dx, dy, dz), GROUPS)
    )


def zp(v):
    return pltpu.roll(v, v.shape[1] - 1, 1)


def zm(v):
    return pltpu.roll(v, 1, 1)


def yp(v):
    return pltpu.roll(v, v.shape[0] - 1, 0)


def ym(v):
    return pltpu.roll(v, 1, 0)


def forward(field):
    modes = {}
    for c in range(3):
        u = field[c]
        up = zp(u)
        for r, w in ((0, u + up), (1, up - u)):
            wp = yp(w)
            modes[c, 0, r] = w + wp
            modes[c, 1, r] = wp - w
    return modes


def across(low, high):
    modes = {}
    for (c, q, r), a in low.items():
        b = high[c, q, r]
        if (q, r) != (0, 0):
            modes[c, 0, q, r] = a + b
        modes[c, 1, q, r] = b - a
    return modes


def stress(u):
    f = {}
    total = (u[0, 1, 0, 0] + u[1, 0, 1, 0] + u[2, 0, 0, 1]) * CROSS
    for c, mode in ((0, (1, 0, 0)), (1, (0, 1, 0)), (2, (0, 0, 1))):
        f[(c,) + mode] = u[(c,) + mode] * (NORMAL - CROSS) + total
    for a, b in (
        ((0, 0, 0, 1), (2, 1, 0, 0)),
        ((0, 0, 1, 0), (1, 1, 0, 0)),
        ((1, 0, 0, 1), (2, 0, 1, 0)),
    ):
        f[a] = f[b] = (u[a] + u[b]) * TWIST
    total = u[0, 0, 1, 1] + u[1, 1, 0, 1] + u[2, 1, 1, 0]
    for a in ((0, 0, 1, 1), (1, 1, 0, 1), (2, 1, 1, 0)):
        f[a] = (u[a] + total) * SPIN
    for a, b in (
        ((0, 1, 0, 1), (1, 0, 1, 1)),
        ((0, 1, 1, 0), (2, 0, 1, 1)),
        ((1, 1, 1, 0), (2, 1, 0, 1)),
    ):
        f[a] = u[a] * BEND + u[b] * BEND_CROSS
        f[b] = u[b] * BEND + u[a] * BEND_CROSS
    for c in range(3):
        f[c, 1, 1, 1] = u[c, 1, 1, 1] * HOUR
    return f


def scaled(f, factor):
    out, seen = {}, {}
    for mode, value in f.items():
        if id(value) not in seen:
            seen[id(value)] = value * factor
        out[mode] = seen[id(value)]
    return out


def backward(modes):
    rows = []
    for c in range(3):
        lines = []
        for r in (0, 1):
            s, d = modes[c, 0, r], modes[c, 1, r]
            lines.append((s - d) + ym(s + d))
        rows.append((lines[0] - lines[1]) + zm(lines[0] + lines[1]))
    return rows


def operator(field, factor, free, span, known, ready):
    result, carry, low = {}, None, None
    for p in span:
        held = [free[p] * u for u in field[p]]
        high = known[p] if p in known else forward(held)
        if low is not None:
            if p - 1 in ready:
                f = ready[p - 1]
            else:
                f = scaled(stress(across(low, high)), factor[p - 1])
            here, later = {}, {}
            for c, q, r in low:
                d = f[c, 1, q, r]
                if (q, r) == (0, 0):
                    here[c, q, r] = -d
                    later[c, q, r] = d
                else:
                    s = f[c, 0, q, r]
                    here[c, q, r] = s - d
                    later[c, q, r] = s + d
            if carry is not None:
                rows = backward({mode: carry[mode] + here[mode] for mode in here})
                result[p - 1] = [
                    free[p - 1] * rows[c] + (field[p - 1][c] - last[c]) for c in range(3)
                ]
            carry = later
        low, last = high, held
    return result


def smooth_plane(v):
    along_z = zp(v) + zm(v)
    along_y = yp(v) + ym(v)
    both = yp(along_z) + ym(along_z)
    sides = along_z + along_y
    return 2.0 * v + EDGE * sides + FACE * both, EDGE * v + FACE * sides + CORNER * both


def smooth(planes):
    parts = [smooth_plane(v) for v in planes]
    return [
        parts[p][0] + (parts[p - 1][1] + parts[p + 1][1]) for p in range(1, len(planes) - 1)
    ]


def block_sum(low, high, even_y, even_z):
    v = low + high
    v = v + jnp.where(even_z, zp(v), zm(v))
    return v + jnp.where(even_y, yp(v), ym(v))


def iota(shape, dim):
    return lax.broadcasted_iota(jnp.int32, shape, dim)


def pack(tiles):
    slot = iota((8, 128), 1) >> 3
    packs = []
    for first in range(0, len(tiles), 16):
        total = None
        for s, tile in enumerate(tiles[first : first + 16]):
            turned = pltpu.roll(tile, (4 + 8 * s) % 128, 1)
            total = turned if total is None else jnp.where(slot == s, turned, total)
        packs.append(total)
    return packs


def unpack(packed, s):
    return pltpu.roll(packed, (124 - 8 * (s % 16)) % 128, 1)


def kernel(
    design_hbm, passive_hbm, fixed_hbm, state_hbm, adjoint_hbm, resid_hbm,
    direction_out, image_out, grads_out, step_out,
    design, passive, fixed, own_sa, in_sem,
    own0, z0, lx0, ly0, lz0, lc0,
    own1, z1, lx1, ly1, lz1, lc1,
    z2, lx2, ly2, lz2, lc2,
    own3, z3, lx3, ly3, lz3, lc3,
    ar_send, ar_land, send_sem, recv_sem, relay_sem,
):
    copies, sent = [], [0]

    def settle():
        for copy in copies[sent[0] :]:
            copy.wait_send()
        sent[0] = len(copies)

    def send(src, dst, target):
        number = len(copies)
        copy = pltpu.make_async_remote_copy(
            src_ref=src,
            dst_ref=dst,
            send_sem=send_sem.at[number],
            recv_sem=recv_sem.at[number],
            device_id=target,
            device_id_type=MESH,
        )
        copy.start()
        copies.append(copy)
        return copy

    def arrive(group):
        for copy in group:
            copy.wait_recv()

    def greet(semaphore, friends):
        for friend in friends:
            pl.semaphore_signal(semaphore, inc=1, device_id=device(*friend), device_id_type=MESH)

    pairs = [(design_hbm, design), (passive_hbm, passive), (fixed_hbm, fixed)]
    for p, first in ((0, 0), (1, 3), (2, 14), (3, 17)):
        pairs.append((resid_hbm.at[:, p], own0.at[pl.ds(first, 3)]))
    pairs += [(adjoint_hbm, own_sa.at[pl.ds(0, 3)]), (state_hbm, own_sa.at[pl.ds(3, 3)])]
    inputs = [pltpu.make_async_copy(src, dst, in_sem.at[n]) for n, (src, dst) in enumerate(pairs)]
    for copy in inputs:
        copy.start()

    barrier = pltpu.get_barrier_semaphore()
    greeted = BOX + [(2, 0, 0), (-2, 0, 0)]
    greet(barrier, greeted)

    place_x, place_y, place_z = (lax.axis_index(axis) for axis in AXES)
    wide = (16, 256)
    row, lane = iota(wide, 0), iota(wide, 1)
    at_y = place_y * 8 + jnp.where(row < 12, row, row - 16)
    at_z = place_z * 128 + jnp.where(lane < 192, lane, lane - 256)
    inside = ((at_y >= 0) & (at_y < 32) & (at_z >= 0) & (at_z < 1024)).astype(jnp.float32)
    inside_low = inside * (place_x > 0).astype(jnp.float32)
    inside_high = inside * (place_x < 23).astype(jnp.float32)

    def sides(dim_at, count):
        return (dim_at > 0).astype(jnp.float32) + (dim_at < count - 1).astype(jnp.float32)

    near_y, near_z = sides(at_y, 32), sides(at_z, 1024)
    near, nearer = near_y + near_z, near_y * near_z
    weight_base = 2.0 + EDGE * near + FACE * nearer
    weight_step = EDGE + FACE * near + CORNER * nearer
    inverse_inner = 1.0 / (weight_base + 2.0 * weight_step)
    inverse_end = 1.0 / (weight_base + weight_step)
    inverse_first = jnp.where(place_x > 0, inverse_inner, inverse_end)
    inverse_last = jnp.where(place_x < 23, inverse_inner, inverse_end)

    def inverse_weight(p):
        return inverse_first if p == 0 else inverse_last if p == 3 else inverse_inner

    even_y, even_z = (row & 1) == 0, (lane & 1) == 0
    tile_even_y, tile_even_z = (iota((8, 128), 0) & 1) == 0, (iota((8, 128), 1) & 1) == 0
    top_half = iota((8, 128), 0) < 4
    low_slot = (iota((8, 128), 1) & 7) < 4

    free_at, masked_at = (6, 7, 8, 13), (9, 10, 11, 12)

    def resid_at(c, p):
        return 3 * p + c + (8 if p > 1 else 0)

    for copy in inputs[:3]:
        copy.wait()
    for p in range(4):
        code = passive[p]
        own0[masked_at[p]] = jnp.where(code == 1, 0.0, jnp.where(code == 2, 1.0, design[p]))
        own0[free_at[p]] = (1 - fixed[p]).astype(jnp.float32)
    for copy in inputs[3:7]:
        copy.wait()
    for n, packed in enumerate(pack([own0[t] for t in range(20)])):
        z0[n] = packed
    pl.semaphore_wait(barrier, len(greeted))

    def exchange(own, edges, land, tiles, packs):
        land_x, land_y, land_z, land_c = land
        near, far = [], []
        for i, j, k in BOX:
            target, slot = device(i, j, k), i + 1
            if k == 0:
                span = pl.ds(*tiles[slot])
                if j == 0:
                    copy = send(own.at[span], land_x.at[slot // 2, span], target)
                else:
                    half = pl.ds(2 * (j + 1), 4)
                    copy = send(own.at[span, half], land_y.at[slot, span, half], target)
            else:
                span = pl.ds(*packs[slot])
                if j == 0:
                    copy = send(edges.at[span], land_z.at[slot, (k + 1) // 2, span], target)
                else:
                    corner = j + 1 + (k + 1) // 2
                    copy = send(edges.at[span], land_c.at[slot, corner, span], target)
            (near if i == 0 else far).append(copy)
        return near, far

    def main_of(own, land, slot, t):
        tile = own[t] if slot == 1 else land[0][slot // 2, t]
        return jnp.concatenate([tile, land[1][slot, t]], 0)

    def edges_of(land, slot, n):
        land_z, land_c = land[2], land[3]
        top = jnp.where(low_slot, land_z[slot, 1, n], land_z[slot, 0, n])
        from_low_y = jnp.where(low_slot, land_c[slot, 3, n], land_c[slot, 2, n])
        from_high_y = jnp.where(low_slot, land_c[slot, 1, n], land_c[slot, 0, n])
        return jnp.concatenate([top, jnp.where(top_half, from_high_y, from_low_y)], 0)

    def widened(main, packed, s):
        return jnp.concatenate([main, unpack(packed, s)], 1)

    masks = (inside_high, inside, inside_low)

    land0 = (lx0, ly0, lz0, lc0)
    near, far = exchange(own0, z0, land0, ((0, 12), (0, 20), (7, 13)), ((0, 1), (0, 2), (0, 2)))
    greet(relay_sem.at[0], [(2, 0, 0), (-2, 0, 0)])
    arrive(near)
    edges0 = {(1, n): edges_of(land0, 1, n) for n in range(2)}

    def input_plane(slot, t):
        return widened(main_of(own0, land0, slot, t), edges0[slot, t // 16], t) * masks[slot]

    masked = {p: input_plane(1, masked_at[p]) for p in range(4)}
    parts = {p: smooth_plane(masked[p]) for p in range(4)}
    free = {p: input_plane(1, free_at[p]) for p in range(4)}
    resid = {p: [input_plane(1, resid_at(c, p)) for c in range(3)] for p in range(4)}
    density, factor, paired = {}, {}, {}
    diagonal, inverse_diag, first = {}, {}, {}
    arrive(far)
    edges0[0, 0] = edges_of(land0, 0, 0)
    for n in range(2):
        edges0[2, n] = edges_of(land0, 2, n)
    greet(relay_sem.at[1], [(0, 0, 2), (0, 0, -2)])
    pl.semaphore_wait(relay_sem.at[0], 2)
    greet(relay_sem.at[2], [(4, 0, 0), (-4, 0, 0)])

    def beyond(p):
        return (2, p + 4) if p < 0 else (0, p - 4)

    def take_masked(p):
        slot, q = beyond(p)
        parts[p] = smooth_plane(input_plane(slot, masked_at[q]))

    def take_nodes(p):
        slot, q = beyond(p)
        free[p] = input_plane(slot, free_at[q])
        if -3 < p < 6:
            resid[p] = [input_plane(slot, resid_at(c, q)) for c in range(3)]

    def take_element(p):
        d = (parts[p][0] + (parts[p - 1][1] + parts[p + 1][1])) * inverse_weight(p)
        density[p] = d
        f = stiff_floor + d * d * d * (1.0 - stiff_floor)
        factor[p] = f * (inside_low if p < 0 else inside if p < 4 else inside_high)
        v = factor[p] + zm(factor[p])
        paired[p] = v + ym(v)

    def take_diagonal(p):
        diagonal[p] = free[p] * (NODE_DIAG * (paired[p] + paired[p - 1])) + (1.0 - free[p])
        inverse_diag[p] = 1.0 / diagonal[p]
        first[p] = [damping * resid[p][c] * inverse_diag[p] for c in range(3)]

    for p in (-3, -2, -1, 4, 5):
        take_masked(p)
    for p in (-1, 4):
        take_nodes(p)
    for p in range(-2, 5):
        if p not in density:
            take_element(p)
    for p in range(-1, 5):
        take_diagonal(p)

    def apply(field, lowest, highest, known=None, ready=None):
        span = range(lowest - 1, highest + 2)
        return operator(field, factor, free, span, known or {}, ready or {})

    image = apply(first, 0, 3)
    second = [
        [(resid[p][c] - image[p][c])[0:8, 0:128] for c in range(3)] for p in range(4)
    ]
    inverse_coarse = {}
    for k in range(2):
        total = block_sum(diagonal[2 * k], diagonal[2 * k + 1], even_y, even_z)
        inverse_coarse[k] = 1.0 / total
    coarse_own = []
    for k in range(2):
        for c in range(3):
            total = block_sum(second[2 * k][c], second[2 * k + 1][c], tile_even_y, tile_even_z)
            coarse_own.append(coarse_damping * total * inverse_coarse[k][0:8, 0:128])
    for t in range(6):
        own1[t] = coarse_own[t]
    z1[0] = pack(coarse_own)[0]
    land1 = (lx1, ly1, lz1, lc1)
    near, far = exchange(own1, z1, land1, ((0, 6),) * 3, ((0, 1),) * 3)

    for copy in inputs[7:]:
        copy.wait()
    for n, packed in enumerate(pack([own_sa[f, p] for p in range(4) for f in range(6)])):
        z2[n] = packed
    top_row = pl.ds(0, 1)
    group2 = [
        send(z2.at[pl.ds(0, 1)], lc2.at[1, pl.ds(0, 1)], device(-1, -1, -1)),
        send(z2, lc2.at[0], device(0, -1, -1)),
        send(z2.at[pl.ds(0, 1)], lz2.at[1, pl.ds(0, 1)], device(-1, 0, -1)),
        send(own_sa.at[:, 0, top_row], ly2.at[:, 4, top_row], device(-1, -1, 0)),
        send(own_sa.at[:, 0], lx2, device(-1, 0, 0)),
        send(own_sa.at[:, :, top_row], ly2.at[:, pl.ds(0, 4), top_row], device(0, -1, 0)),
        send(z2, lz2.at[0], device(0, 0, -1)),
    ]
    pl.semaphore_wait(relay_sem.at[2], 2)
    greet(relay_sem.at[3], [(8, 0, 0), (-8, 0, 0)])
    for p in (-4, 6):
        take_masked(p)
    for p in (-3, -2, 5, 6):
        take_nodes(p)
    for p in (-3, 5):
        take_element(p)
    for p in (-2, 5):
        take_diagonal(p)
    for k in (-1, 2):
        total = block_sum(diagonal[2 * k], diagonal[2 * k + 1], even_y, even_z)
        inverse_coarse[k] = 1.0 / total

    arrive(near)
    coarse = {}

    def coarse_plane(slot, k):
        edges = edges_of(land1, slot, 0)
        return [
            widened(main_of(own1, land1, slot, 3 * k + c), edges, 3 * k + c) * masks[slot]
            for c in range(3)
        ]

    for k in range(2):
        coarse[k] = coarse_plane(1, k)
    known = {p: forward([free[p] * u for u in coarse[p // 2]]) for p in range(4)}
    ready = {p: scaled(stress(across(known[p], known[p + 1])), factor[p]) for p in range(3)}
    arrive(far)
    for k in range(2):
        coarse[k - 2] = coarse_plane(2, k)
        coarse[k + 2] = coarse_plane(0, k)
    pl.semaphore_wait(relay_sem.at[1], 2)
    spread = {p: coarse[p // 2] for p in range(-4, 8)}
    image = apply(spread, -2, 5, known, ready)
    middle = {}
    for k in range(-1, 3):
        for c in range(3):
            total = block_sum(image[2 * k][c], image[2 * k + 1][c], even_y, even_z)
            fix = 2.0 * coarse[k][c] - coarse_damping * total * inverse_coarse[k]
            for p in (2 * k, 2 * k + 1):
                middle.setdefault(p, []).append(first[p][c] + fix)
    direction = {}

    def smoothed_again(lowest, highest):
        image = apply(middle, lowest, highest)
        for p in range(lowest, highest + 1):
            direction[p] = [
                middle[p][c] + damping * (resid[p][c] - image[p][c]) * inverse_diag[p]
                for c in range(3)
            ]

    smoothed_again(0, 4)
    held_modes = {p: forward([free[p] * d for d in direction[p]]) for p in range(5)}
    numerator = denominator = None
    for p in range(4):
        u = across(*({m: v[0:8, 0:128] for m, v in held_modes[p + n].items()} for n in range(2)))
        energy = None
        for mode, value in stress(u).items():
            term = u[mode] * value
            energy = term if energy is None else energy + term
        b = factor[p][0:8, 0:128] * energy
        fixed_part = None
        for c in range(3):
            d = direction[p][c][0:8, 0:128]
            direction_out[c, p] = d
            a = resid[p][c][0:8, 0:128] * d
            numerator = a if numerator is None else numerator + a
            fixed_part = d * d if fixed_part is None else fixed_part + d * d
        b = b + (1.0 - free[p][0:8, 0:128]) * fixed_part
        denominator = b if denominator is None else denominator + b
    numerator = jnp.sum(numerator, axis=0, keepdims=True)
    denominator = jnp.sum(denominator, axis=0, keepdims=True)
    sums = jnp.concatenate([numerator, denominator], 0)

    landed = [0]
    pair = pl.ds(0, 2)

    def spread_sums(stage, value, targets):
        ar_send[stage, 0:2] = value
        base = landed[0]
        landed[0] += len(targets)
        group = [
            send(ar_send.at[stage, pair], ar_land.at[base + n, pair], target)
            for n, target in enumerate(targets)
        ]

        def gather():
            arrive(group)
            total = value
            for n in range(len(targets)):
                total = total + ar_land[base + n, 0:2]
            return total

        return gather

    gather = spread_sums(0, sums, [device(0, j, k) for j, k in FLAT])
    arrive(group2)

    edges2 = [jnp.concatenate([lz2[0, n], lc2[0, n]], 0) for n in range(2)]
    edges2_high = jnp.concatenate([lz2[1, 0], lc2[1, 0]], 0)

    def ends(f, p):
        if p < 4:
            main = jnp.concatenate([own_sa[f, p], ly2[f, p]], 0)
            return widened(main, edges2[(6 * p + f) // 16], 6 * p + f) * inside
        main = jnp.concatenate([lx2[f], ly2[f, 4]], 0)
        return widened(main, edges2_high, f) * inside_high

    def corner_modes(fields):
        return [{m: v[0:8, 0:128] for m, v in forward(fields[p]).items()} for p in range(5)]

    adjoint_modes = corner_modes([[ends(c, p) for c in range(3)] for p in range(5)])
    state_modes = corner_modes([[ends(3 + c, p) for c in range(3)] for p in range(5)])
    direction_modes = corner_modes([direction[p] for p in range(5)])
    sens = []
    for p in range(4):
        force = stress(across(state_modes[p], state_modes[p + 1]))
        d = density[p][0:8, 0:128]
        weight = 3.0 * (1.0 - stiff_floor) * d * d * inverse_weight(p)[0:8, 0:128]
        for modes in (adjoint_modes, direction_modes):
            with_modes = across(modes[p], modes[p + 1])
            energy = None
            for mode, value in force.items():
                term = with_modes[mode] * value
                energy = term if energy is None else energy + term
            sens.append(weight * energy)
    for t in range(8):
        own3[t] = sens[t]
    z3[0] = pack(sens)[0]
    land3 = (lx3, ly3, lz3, lc3)
    settle()
    near, far = exchange(own3, z3, land3, ((0, 2), (0, 8), (6, 2)), ((0, 1),) * 3)
    smoothed_again(-1, -1)
    image = apply(direction, 0, 3, held_modes)
    for p in range(4):
        for c in range(3):
            image_out[c, p] = image[p][c][0:8, 0:128]
    sums = gather()
    pl.semaphore_wait(relay_sem.at[3], 2)
    gather = spread_sums(1, sums, [device(i, 0, 0) for i in LINE])
    arrive(near)
    arrive(far)
    edges3 = [edges_of(land3, slot, 0) for slot in range(3)]

    def sens_plane(slot, t):
        return widened(main_of(own3, land3, slot, t), edges3[slot], t) * masks[slot]

    for f in range(2):
        planes = [sens_plane(2, 6 + f)]
        planes += [sens_plane(1, 2 * p + f) for p in range(4)]
        planes += [sens_plane(0, f)]
        for p, v in enumerate(smooth(planes)):
            grads_out[f, p] = v[0:8, 0:128]
    settle()
    sums = gather()
    sums = jnp.sum(sums, axis=1, keepdims=True)
    step_out[...] = jnp.broadcast_to(sums[0:1] / sums[1:2], (8, 128))
    settle()


def body(design, passive, fixed, state, adjoint, resid):
    def scratch(*shape):
        return pltpu.VMEM(shape, jnp.float32)

    def landing(tiles, packs):
        return [
            scratch(2, tiles, 8, 128),
            scratch(3, tiles, 8, 128),
            scratch(3, 2, packs, 8, 128),
            scratch(3, 4, packs, 8, 128),
        ]

    n_copies = 3 * 26 + 7 + 54
    direction, image, grads, step = pl.pallas_call(
        kernel,
        out_shape=(
            pltpu.VMEM((3, 4, 8, 128), jnp.float32),
            pltpu.VMEM((3, 4, 8, 128), jnp.float32),
            pltpu.VMEM((2, 4, 8, 128), jnp.float32),
            pltpu.VMEM((8, 128), jnp.float32),
        ),
        in_specs=[pl.BlockSpec(memory_space=pl.ANY)] * 6,
        out_specs=(pl.BlockSpec(memory_space=pltpu.VMEM),) * 4,
        scratch_shapes=[
            scratch(4, 8, 128),
            pltpu.VMEM((4, 8, 128), jnp.int32),
            pltpu.VMEM((4, 8, 128), jnp.int32),
            scratch(6, 4, 8, 128),
            pltpu.SemaphoreType.DMA((9,)),
            scratch(20, 8, 128),
            scratch(2, 8, 128),
            *landing(20, 2),
            scratch(6, 8, 128),
            scratch(1, 8, 128),
            *landing(6, 1),
            scratch(2, 8, 128),
            scratch(6, 8, 128),
            scratch(6, 5, 8, 128),
            scratch(2, 2, 8, 128),
            scratch(2, 2, 8, 128),
            scratch(8, 8, 128),
            scratch(1, 8, 128),
            *landing(8, 1),
            scratch(2, 8, 128),
            scratch(54, 8, 128),
            pltpu.SemaphoreType.DMA((n_copies,)),
            pltpu.SemaphoreType.DMA((n_copies,)),
            pltpu.SemaphoreType.REGULAR((4,)),
        ],
        compiler_params=pltpu.CompilerParams(
            collective_id=0, has_side_effects=True, vmem_limit_bytes=62 * 2**20
        ),
    )(design, passive, fixed, state, adjoint, resid)
    return (
        adjoint + step * direction,
        resid - step * image,
        jnp.where(passive == 0, grads[0] + step * grads[1], 0.0),
    )


def solution(mesh):
    return jax.shard_map(
        body,
        mesh=mesh,
        in_specs=(P("gx", "gy", "gz"),) * 3 + (P(None, "gx", "gy", "gz"),) * 3,
        out_specs=(P(None, "gx", "gy", "gz"), P(None, "gx", "gy", "gz"), P("gx", "gy", "gz")),
        check_vma=False,
    )
```

```python
import math

import jax
import jax.numpy as jnp
from jax import lax
from jax.experimental import pallas as pl
from jax.experimental.pallas import tpu as pltpu
from jax.sharding import PartitionSpec as P

stiff_floor = 0.001
damping = 0.6
coarse_damping = 0.5

MESH = pl.DeviceIdType.MESH
AXES = ("gx", "gy", "gz")
GROUPS = (24, 4, 8)
EDGE = 1.0
FACE = 2.0 - math.sqrt(2.0)
CORNER = 2.0 - math.sqrt(3.0)

LAME = 0.3 / (1.3 * 0.4)
SHEAR = 0.5 / 1.3
NORMAL = (LAME + 2.0 * SHEAR) / 16.0
CROSS = LAME / 16.0
TWIST = SHEAR / 16.0
BEND = (LAME + 2.0 * SHEAR + SHEAR) / 48.0
BEND_CROSS = LAME / 48.0
SPIN = SHEAR / 48.0
HOUR = (LAME + 2.0 * SHEAR + 2.0 * SHEAR) / 144.0
NODE_DIAG = (LAME + 2.0 * SHEAR + 2.0 * SHEAR) / 9.0

BOX = [(i, j, k) for i in (-1, 0, 1) for j in (-1, 0, 1) for k in (-1, 0, 1)]
BOX = sorted((b for b in BOX if any(b)), key=lambda b: (-sum(map(abs, b)), b[0] == 0))

FLAT = [(j, k) for j in range(4) for k in range(8) if j or k]
FLAT.sort(key=lambda t: -min(t[0], 4 - t[0]) - min(t[1], 8 - t[1]))
LINE = sorted(range(1, 24), key=lambda i: -min(i, 24 - i))


def device(dx, dy, dz):
    return tuple(
        lax.rem(lax.axis_index(axis) + (step + count), count)
        for axis, step, count in zip(AXES, (dx, dy, dz), GROUPS)
    )


def zp(v):
    return pltpu.roll(v, v.shape[1] - 1, 1)


def zm(v):
    return pltpu.roll(v, 1, 1)


def yp(v):
    return pltpu.roll(v, v.shape[0] - 1, 0)


def ym(v):
    return pltpu.roll(v, 1, 0)


def forward(field):
    modes = {}
    for c in range(3):
        u = field[c]
        up = zp(u)
        for r, w in ((0, u + up), (1, up - u)):
            wp = yp(w)
            modes[c, 0, r] = w + wp
            modes[c, 1, r] = wp - w
    return modes


def across(low, high):
    modes = {}
    for (c, q, r), a in low.items():
        b = high[c, q, r]
        if (q, r) != (0, 0):
            modes[c, 0, q, r] = a + b
        modes[c, 1, q, r] = b - a
    return modes


def stress(u):
    f = {}
    total = (u[0, 1, 0, 0] + u[1, 0, 1, 0] + u[2, 0, 0, 1]) * CROSS
    for c, mode in ((0, (1, 0, 0)), (1, (0, 1, 0)), (2, (0, 0, 1))):
        f[(c,) + mode] = u[(c,) + mode] * (NORMAL - CROSS) + total
    for a, b in (
        ((0, 0, 0, 1), (2, 1, 0, 0)),
        ((0, 0, 1, 0), (1, 1, 0, 0)),
        ((1, 0, 0, 1), (2, 0, 1, 0)),
    ):
        f[a] = f[b] = (u[a] + u[b]) * TWIST
    total = u[0, 0, 1, 1] + u[1, 1, 0, 1] + u[2, 1, 1, 0]
    for a in ((0, 0, 1, 1), (1, 1, 0, 1), (2, 1, 1, 0)):
        f[a] = (u[a] + total) * SPIN
    for a, b in (
        ((0, 1, 0, 1), (1, 0, 1, 1)),
        ((0, 1, 1, 0), (2, 0, 1, 1)),
        ((1, 1, 1, 0), (2, 1, 0, 1)),
    ):
        f[a] = u[a] * BEND + u[b] * BEND_CROSS
        f[b] = u[b] * BEND + u[a] * BEND_CROSS
    for c in range(3):
        f[c, 1, 1, 1] = u[c, 1, 1, 1] * HOUR
    return f


def scaled(f, factor):
    out, seen = {}, {}
    for mode, value in f.items():
        if id(value) not in seen:
            seen[id(value)] = value * factor
        out[mode] = seen[id(value)]
    return out


def backward(modes):
    rows = []
    for c in range(3):
        lines = []
        for r in (0, 1):
            s, d = modes[c, 0, r], modes[c, 1, r]
            lines.append((s - d) + ym(s + d))
        rows.append((lines[0] - lines[1]) + zm(lines[0] + lines[1]))
    return rows


def operator(field, factor, free, span, known, ready):
    result, carry, low = {}, None, None
    for p in span:
        held = [free[p] * u for u in field[p]]
        high = known[p] if p in known else forward(held)
        if low is not None:
            if p - 1 in ready:
                f = ready[p - 1]
            else:
                f = scaled(stress(across(low, high)), factor[p - 1])
            here, later = {}, {}
            for c, q, r in low:
                d = f[c, 1, q, r]
                if (q, r) == (0, 0):
                    here[c, q, r] = -d
                    later[c, q, r] = d
                else:
                    s = f[c, 0, q, r]
                    here[c, q, r] = s - d
                    later[c, q, r] = s + d
            if carry is not None:
                rows = backward({mode: carry[mode] + here[mode] for mode in here})
                result[p - 1] = [
                    free[p - 1] * rows[c] + (field[p - 1][c] - last[c]) for c in range(3)
                ]
            carry = later
        low, last = high, held
    return result


def smooth_plane(v):
    along_z = zp(v) + zm(v)
    along_y = yp(v) + ym(v)
    both = yp(along_z) + ym(along_z)
    sides = along_z + along_y
    return 2.0 * v + EDGE * sides + FACE * both, EDGE * v + FACE * sides + CORNER * both


def smooth(planes):
    parts = [smooth_plane(v) for v in planes]
    return [
        parts[p][0] + (parts[p - 1][1] + parts[p + 1][1]) for p in range(1, len(planes) - 1)
    ]


def block_sum(low, high, even_y, even_z):
    v = low + high
    v = v + jnp.where(even_z, zp(v), zm(v))
    return v + jnp.where(even_y, yp(v), ym(v))


def iota(shape, dim):
    return lax.broadcasted_iota(jnp.int32, shape, dim)


def pack(tiles):
    slot = iota((8, 128), 1) >> 3
    packs = []
    for first in range(0, len(tiles), 16):
        total = None
        for s, tile in enumerate(tiles[first : first + 16]):
            turned = pltpu.roll(tile, (4 + 8 * s) % 128, 1)
            total = turned if total is None else jnp.where(slot == s, turned, total)
        packs.append(total)
    return packs


def unpack(packed, s):
    return pltpu.roll(packed, (124 - 8 * (s % 16)) % 128, 1)


def kernel(
    design_hbm, passive_hbm, fixed_hbm, state_hbm, adjoint_hbm, resid_hbm,
    direction_out, image_out, grads_out, step_out,
    design, passive, fixed, own_sa, in_sem,
    own0, z0, lx0, ly0, lz0, lc0,
    own1, z1, lx1, ly1, lz1, lc1,
    z2, lx2, ly2, lz2, lc2,
    own3, z3, lx3, ly3, lz3, lc3,
    ar_send, ar_land, send_sem, recv_sem, relay_sem,
):
    copies, sent = [], [0]

    def settle():
        for copy in copies[sent[0] :]:
            copy.wait_send()
        sent[0] = len(copies)

    def send(src, dst, target):
        number = len(copies)
        copy = pltpu.make_async_remote_copy(
            src_ref=src,
            dst_ref=dst,
            send_sem=send_sem.at[number],
            recv_sem=recv_sem.at[number],
            device_id=target,
            device_id_type=MESH,
        )
        copy.start()
        copies.append(copy)
        return copy

    def arrive(group):
        for copy in group:
            copy.wait_recv()

    def greet(semaphore, friends):
        for friend in friends:
            pl.semaphore_signal(semaphore, inc=1, device_id=device(*friend), device_id_type=MESH)

    pairs = [(design_hbm, design), (passive_hbm, passive), (fixed_hbm, fixed)]
    for p, first in ((0, 0), (1, 3), (2, 14), (3, 17)):
        pairs.append((resid_hbm.at[:, p], own0.at[pl.ds(first, 3)]))
    pairs += [(adjoint_hbm, own_sa.at[pl.ds(0, 3)]), (state_hbm, own_sa.at[pl.ds(3, 3)])]
    inputs = [pltpu.make_async_copy(src, dst, in_sem.at[n]) for n, (src, dst) in enumerate(pairs)]
    for copy in inputs:
        copy.start()

    barrier = pltpu.get_barrier_semaphore()
    greeted = BOX + [(2, 0, 0), (-2, 0, 0)]
    greet(barrier, greeted)

    place_x, place_y, place_z = (lax.axis_index(axis) for axis in AXES)
    wide = (16, 256)
    row, lane = iota(wide, 0), iota(wide, 1)
    at_y = place_y * 8 + jnp.where(row < 12, row, row - 16)
    at_z = place_z * 128 + jnp.where(lane < 192, lane, lane - 256)
    inside = ((at_y >= 0) & (at_y < 32) & (at_z >= 0) & (at_z < 1024)).astype(jnp.float32)
    inside_low = inside * (place_x > 0).astype(jnp.float32)
    inside_high = inside * (place_x < 23).astype(jnp.float32)

    def sides(dim_at, count):
        return (dim_at > 0).astype(jnp.float32) + (dim_at < count - 1).astype(jnp.float32)

    near_y, near_z = sides(at_y, 32), sides(at_z, 1024)
    near, nearer = near_y + near_z, near_y * near_z
    weight_base = 2.0 + EDGE * near + FACE * nearer
    weight_step = EDGE + FACE * near + CORNER * nearer
    inverse_inner = 1.0 / (weight_base + 2.0 * weight_step)
    inverse_end = 1.0 / (weight_base + weight_step)
    inverse_first = jnp.where(place_x > 0, inverse_inner, inverse_end)
    inverse_last = jnp.where(place_x < 23, inverse_inner, inverse_end)

    def inverse_weight(p):
        return inverse_first if p == 0 else inverse_last if p == 3 else inverse_inner

    even_y, even_z = (row & 1) == 0, (lane & 1) == 0
    tile_even_y, tile_even_z = (iota((8, 128), 0) & 1) == 0, (iota((8, 128), 1) & 1) == 0
    top_half = iota((8, 128), 0) < 4
    low_slot = (iota((8, 128), 1) & 7) < 4

    free_at, masked_at = (6, 7, 8, 13), (9, 10, 11, 12)

    def resid_at(c, p):
        return 3 * p + c + (8 if p > 1 else 0)

    for copy in inputs[:3]:
        copy.wait()
    for p in range(4):
        code = passive[p]
        own0[masked_at[p]] = jnp.where(code == 1, 0.0, jnp.where(code == 2, 1.0, design[p]))
        own0[free_at[p]] = (1 - fixed[p]).astype(jnp.float32)
    for copy in inputs[3:7]:
        copy.wait()
    for n, packed in enumerate(pack([own0[t] for t in range(20)])):
        z0[n] = packed
    pl.semaphore_wait(barrier, len(greeted))

    def exchange(own, edges, land, tiles, packs):
        land_x, land_y, land_z, land_c = land
        near, far = [], []
        for i, j, k in BOX:
            target, slot = device(i, j, k), i + 1
            if k == 0:
                span = pl.ds(*tiles[slot])
                if j == 0:
                    copy = send(own.at[span], land_x.at[slot // 2, span], target)
                else:
                    half = pl.ds(2 * (j + 1), 4)
                    copy = send(own.at[span, half], land_y.at[slot, span, half], target)
            else:
                span = pl.ds(*packs[slot])
                if j == 0:
                    copy = send(edges.at[span], land_z.at[slot, (k + 1) // 2, span], target)
                else:
                    corner = j + 1 + (k + 1) // 2
                    half = pl.ds(2 * (j + 1), 4)
                    copy = send(edges.at[span, half], land_c.at[slot, corner, span, half], target)
            (near if i == 0 else far).append(copy)
        return near, far

    def main_of(own, land, slot, t):
        tile = own[t] if slot == 1 else land[0][slot // 2, t]
        return jnp.concatenate([tile, land[1][slot, t]], 0)

    def edges_of(land, slot, n):
        land_z, land_c = land[2], land[3]
        top = jnp.where(low_slot, land_z[slot, 1, n], land_z[slot, 0, n])
        from_low_y = jnp.where(low_slot, land_c[slot, 3, n], land_c[slot, 2, n])
        from_high_y = jnp.where(low_slot, land_c[slot, 1, n], land_c[slot, 0, n])
        return jnp.concatenate([top, jnp.where(top_half, from_high_y, from_low_y)], 0)

    def widened(main, packed, s):
        return jnp.concatenate([main, unpack(packed, s)], 1)

    masks = (inside_high, inside, inside_low)

    land0 = (lx0, ly0, lz0, lc0)
    near, far = exchange(own0, z0, land0, ((0, 12), (0, 20), (7, 13)), ((0, 1), (0, 2), (0, 2)))
    greet(relay_sem.at[0], [(2, 0, 0), (-2, 0, 0)])
    arrive(near)
    edges0 = {(1, n): edges_of(land0, 1, n) for n in range(2)}

    def input_plane(slot, t):
        return widened(main_of(own0, land0, slot, t), edges0[slot, t // 16], t) * masks[slot]

    masked = {p: input_plane(1, masked_at[p]) for p in range(4)}
    parts = {p: smooth_plane(masked[p]) for p in range(4)}
    free = {p: input_plane(1, free_at[p]) for p in range(4)}
    resid = {p: [input_plane(1, resid_at(c, p)) for c in range(3)] for p in range(4)}
    density, factor, paired = {}, {}, {}
    diagonal, inverse_diag, first = {}, {}, {}
    arrive(far)
    edges0[0, 0] = edges_of(land0, 0, 0)
    for n in range(2):
        edges0[2, n] = edges_of(land0, 2, n)
    greet(relay_sem.at[1], [(0, 0, 2), (0, 0, -2)])
    pl.semaphore_wait(relay_sem.at[0], 2)
    greet(relay_sem.at[2], [(4, 0, 0), (-4, 0, 0)])

    def beyond(p):
        return (2, p + 4) if p < 0 else (0, p - 4)

    def take_masked(p):
        slot, q = beyond(p)
        parts[p] = smooth_plane(input_plane(slot, masked_at[q]))

    def take_nodes(p):
        slot, q = beyond(p)
        free[p] = input_plane(slot, free_at[q])
        if -3 < p < 6:
            resid[p] = [input_plane(slot, resid_at(c, q)) for c in range(3)]

    def take_element(p):
        d = (parts[p][0] + (parts[p - 1][1] + parts[p + 1][1])) * inverse_weight(p)
        density[p] = d
        f = stiff_floor + d * d * d * (1.0 - stiff_floor)
        factor[p] = f * (inside_low if p < 0 else inside if p < 4 else inside_high)
        v = factor[p] + zm(factor[p])
        paired[p] = v + ym(v)

    def take_diagonal(p):
        diagonal[p] = free[p] * (NODE_DIAG * (paired[p] + paired[p - 1])) + (1.0 - free[p])
        inverse_diag[p] = 1.0 / diagonal[p]
        first[p] = [damping * resid[p][c] * inverse_diag[p] for c in range(3)]

    for p in (-3, -2, -1, 4, 5):
        take_masked(p)
    for p in (-1, 4):
        take_nodes(p)
    for p in range(-2, 5):
        if p not in density:
            take_element(p)
    for p in range(-1, 5):
        take_diagonal(p)

    def apply(field, lowest, highest, known=None, ready=None):
        span = range(lowest - 1, highest + 2)
        return operator(field, factor, free, span, known or {}, ready or {})

    image = apply(first, 0, 3)
    second = [
        [(resid[p][c] - image[p][c])[0:8, 0:128] for c in range(3)] for p in range(4)
    ]
    inverse_coarse = {}
    for k in range(2):
        total = block_sum(diagonal[2 * k], diagonal[2 * k + 1], even_y, even_z)
        inverse_coarse[k] = 1.0 / total
    coarse_own = []
    for k in range(2):
        for c in range(3):
            total = block_sum(second[2 * k][c], second[2 * k + 1][c], tile_even_y, tile_even_z)
            coarse_own.append(coarse_damping * total * inverse_coarse[k][0:8, 0:128])
    for t in range(6):
        own1[t] = coarse_own[t]
    z1[0] = pack(coarse_own)[0]
    land1 = (lx1, ly1, lz1, lc1)
    near, far = exchange(own1, z1, land1, ((0, 6),) * 3, ((0, 1),) * 3)

    for copy in inputs[7:]:
        copy.wait()
    for n, packed in enumerate(pack([own_sa[f, p] for p in range(4) for f in range(6)])):
        z2[n] = packed
    top_row = pl.ds(0, 1)
    group2 = [
        send(z2.at[pl.ds(0, 1)], lc2.at[1, pl.ds(0, 1)], device(-1, -1, -1)),
        send(z2, lc2.at[0], device(0, -1, -1)),
        send(z2.at[pl.ds(0, 1)], lz2.at[1, pl.ds(0, 1)], device(-1, 0, -1)),
        send(own_sa.at[:, 0, top_row], ly2.at[:, 4, top_row], device(-1, -1, 0)),
        send(own_sa.at[:, 0], lx2, device(-1, 0, 0)),
        send(own_sa.at[:, :, top_row], ly2.at[:, pl.ds(0, 4), top_row], device(0, -1, 0)),
        send(z2, lz2.at[0], device(0, 0, -1)),
    ]
    pl.semaphore_wait(relay_sem.at[2], 2)
    greet(relay_sem.at[3], [(8, 0, 0), (-8, 0, 0)])
    for p in (-4, 6):
        take_masked(p)
    for p in (-3, -2, 5, 6):
        take_nodes(p)
    for p in (-3, 5):
        take_element(p)
    for p in (-2, 5):
        take_diagonal(p)
    for k in (-1, 2):
        total = block_sum(diagonal[2 * k], diagonal[2 * k + 1], even_y, even_z)
        inverse_coarse[k] = 1.0 / total

    arrive(near)
    coarse = {}

    def coarse_plane(slot, k):
        edges = edges_of(land1, slot, 0)
        return [
            widened(main_of(own1, land1, slot, 3 * k + c), edges, 3 * k + c) * masks[slot]
            for c in range(3)
        ]

    for k in range(2):
        coarse[k] = coarse_plane(1, k)
    known = {p: forward([free[p] * u for u in coarse[p // 2]]) for p in range(4)}
    ready = {p: scaled(stress(across(known[p], known[p + 1])), factor[p]) for p in range(3)}
    arrive(far)
    for k in range(2):
        coarse[k - 2] = coarse_plane(2, k)
        coarse[k + 2] = coarse_plane(0, k)
    pl.semaphore_wait(relay_sem.at[1], 2)
    spread = {p: coarse[p // 2] for p in range(-4, 8)}
    image = apply(spread, -2, 5, known, ready)
    middle = {}
    for k in range(-1, 3):
        for c in range(3):
            total = block_sum(image[2 * k][c], image[2 * k + 1][c], even_y, even_z)
            fix = 2.0 * coarse[k][c] - coarse_damping * total * inverse_coarse[k]
            for p in (2 * k, 2 * k + 1):
                middle.setdefault(p, []).append(first[p][c] + fix)
    direction = {}

    def smoothed_again(lowest, highest):
        image = apply(middle, lowest, highest)
        for p in range(lowest, highest + 1):
            direction[p] = [
                middle[p][c] + damping * (resid[p][c] - image[p][c]) * inverse_diag[p]
                for c in range(3)
            ]

    smoothed_again(0, 4)
    held_modes = {p: forward([free[p] * d for d in direction[p]]) for p in range(5)}
    numerator = denominator = None
    for p in range(4):
        u = across(*({m: v[0:8, 0:128] for m, v in held_modes[p + n].items()} for n in range(2)))
        energy = None
        for mode, value in stress(u).items():
            term = u[mode] * value
            energy = term if energy is None else energy + term
        b = factor[p][0:8, 0:128] * energy
        fixed_part = None
        for c in range(3):
            d = direction[p][c][0:8, 0:128]
            direction_out[c, p] = d
            a = resid[p][c][0:8, 0:128] * d
            numerator = a if numerator is None else numerator + a
            fixed_part = d * d if fixed_part is None else fixed_part + d * d
        b = b + (1.0 - free[p][0:8, 0:128]) * fixed_part
        denominator = b if denominator is None else denominator + b
    sums = jnp.where(
        iota((8, 128), 1) < 64,
        numerator + pltpu.roll(numerator, 64, 1),
        denominator + pltpu.roll(denominator, 64, 1),
    )
    sums = jnp.sum(sums, axis=0, keepdims=True)

    landed = [0]
    pair = pl.ds(0, 1)

    def spread_sums(stage, value, targets):
        ar_send[stage, 0:1] = value
        base = landed[0]
        landed[0] += len(targets)
        group = [
            send(ar_send.at[stage, pair], ar_land.at[base + n, pair], target)
            for n, target in enumerate(targets)
        ]

        def gather():
            arrive(group)
            total = value
            for n in range(len(targets)):
                total = total + ar_land[base + n, 0:1]
            return total

        return gather

    gather = spread_sums(0, sums, [device(0, j, k) for j, k in FLAT])
    arrive(group2)

    edges2 = [jnp.concatenate([lz2[0, n], lc2[0, n]], 0) for n in range(2)]
    edges2_high = jnp.concatenate([lz2[1, 0], lc2[1, 0]], 0)

    def ends(f, p):
        if p < 4:
            main = jnp.concatenate([own_sa[f, p], ly2[f, p]], 0)
            return widened(main, edges2[(6 * p + f) // 16], 6 * p + f) * inside
        main = jnp.concatenate([lx2[f], ly2[f, 4]], 0)
        return widened(main, edges2_high, f) * inside_high

    def corner_modes(fields):
        return [{m: v[0:8, 0:128] for m, v in forward(fields[p]).items()} for p in range(5)]

    adjoint_modes = corner_modes([[ends(c, p) for c in range(3)] for p in range(5)])
    state_modes = corner_modes([[ends(3 + c, p) for c in range(3)] for p in range(5)])
    direction_modes = corner_modes([direction[p] for p in range(5)])
    sens = []
    for p in range(4):
        force = stress(across(state_modes[p], state_modes[p + 1]))
        d = density[p][0:8, 0:128]
        weight = 3.0 * (1.0 - stiff_floor) * d * d * inverse_weight(p)[0:8, 0:128]
        for modes in (adjoint_modes, direction_modes):
            with_modes = across(modes[p], modes[p + 1])
            energy = None
            for mode, value in force.items():
                term = with_modes[mode] * value
                energy = term if energy is None else energy + term
            sens.append(weight * energy)
    for t in range(8):
        own3[t] = sens[t]
    z3[0] = pack(sens)[0]
    land3 = (lx3, ly3, lz3, lc3)
    settle()
    near, far = exchange(own3, z3, land3, ((0, 2), (0, 8), (6, 2)), ((0, 1),) * 3)
    smoothed_again(-1, -1)
    image = apply(direction, 0, 3, held_modes)
    for p in range(4):
        for c in range(3):
            image_out[c, p] = image[p][c][0:8, 0:128]
    sums = gather()
    pl.semaphore_wait(relay_sem.at[3], 2)
    gather = spread_sums(1, sums, [device(i, 0, 0) for i in LINE])
    arrive(near)
    arrive(far)
    edges3 = [edges_of(land3, slot, 0) for slot in range(3)]

    def sens_plane(slot, t):
        return widened(main_of(own3, land3, slot, t), edges3[slot], t) * masks[slot]

    for f in range(2):
        planes = [sens_plane(2, 6 + f)]
        planes += [sens_plane(1, 2 * p + f) for p in range(4)]
        planes += [sens_plane(0, f)]
        for p, v in enumerate(smooth(planes)):
            grads_out[f, p] = v[0:8, 0:128]
    settle()
    sums = gather()
    first_half = iota((1, 128), 1) < 64
    numerator = jnp.sum(jnp.where(first_half, sums, 0.0), axis=1, keepdims=True)
    denominator = jnp.sum(jnp.where(first_half, 0.0, sums), axis=1, keepdims=True)
    step_out[...] = jnp.broadcast_to(numerator / denominator, (8, 128))
    settle()


def body(design, passive, fixed, state, adjoint, resid):
    def scratch(*shape):
        return pltpu.VMEM(shape, jnp.float32)

    def landing(tiles, packs):
        return [
            scratch(2, tiles, 8, 128),
            scratch(3, tiles, 8, 128),
            scratch(3, 2, packs, 8, 128),
            scratch(3, 4, packs, 8, 128),
        ]

    n_copies = 3 * 26 + 7 + 54
    direction, image, grads, step = pl.pallas_call(
        kernel,
        out_shape=(
            pltpu.VMEM((3, 4, 8, 128), jnp.float32),
            pltpu.VMEM((3, 4, 8, 128), jnp.float32),
            pltpu.VMEM((2, 4, 8, 128), jnp.float32),
            pltpu.VMEM((8, 128), jnp.float32),
        ),
        in_specs=[pl.BlockSpec(memory_space=pl.ANY)] * 6,
        out_specs=(pl.BlockSpec(memory_space=pltpu.VMEM),) * 4,
        scratch_shapes=[
            scratch(4, 8, 128),
            pltpu.VMEM((4, 8, 128), jnp.int32),
            pltpu.VMEM((4, 8, 128), jnp.int32),
            scratch(6, 4, 8, 128),
            pltpu.SemaphoreType.DMA((9,)),
            scratch(20, 8, 128),
            scratch(2, 8, 128),
            *landing(20, 2),
            scratch(6, 8, 128),
            scratch(1, 8, 128),
            *landing(6, 1),
            scratch(2, 8, 128),
            scratch(6, 8, 128),
            scratch(6, 5, 8, 128),
            scratch(2, 2, 8, 128),
            scratch(2, 2, 8, 128),
            scratch(8, 8, 128),
            scratch(1, 8, 128),
            *landing(8, 1),
            scratch(2, 8, 128),
            scratch(54, 8, 128),
            pltpu.SemaphoreType.DMA((n_copies,)),
            pltpu.SemaphoreType.DMA((n_copies,)),
            pltpu.SemaphoreType.REGULAR((4,)),
        ],
        compiler_params=pltpu.CompilerParams(
            collective_id=0, has_side_effects=True, vmem_limit_bytes=62 * 2**20
        ),
    )(design, passive, fixed, state, adjoint, resid)
    return (
        adjoint + step * direction,
        resid - step * image,
        jnp.where(passive == 0, grads[0] + step * grads[1], 0.0),
    )


def solution(mesh):
    return jax.shard_map(
        body,
        mesh=mesh,
        in_specs=(P("gx", "gy", "gz"),) * 3 + (P(None, "gx", "gy", "gz"),) * 3,
        out_specs=(P(None, "gx", "gy", "gz"), P(None, "gx", "gy", "gz"), P("gx", "gy", "gz")),
        check_vma=False,
    )
```
